32 devices in a mesh: groups: 2 (over y), tensor: 4 (over z), enc: 2 (over x), req: 2 (over core).
Axes of the slice: x: 2, y: 2, z: 4, core: 2. Of those that a mesh axis runs over, the one named last changes fastest.
Arguments:
- span_tokens: bfloat16 [8192, 1024], P(('groups', 'enc', 'req')), parts along dimension 0, may hold values from -6 to 6
- span_request: int32 [512, 1], P('groups'), parts along dimension 0, may hold values from 0 to 31; in each aligned block of 64 rows (0 to 63, 64 to 127, ...) at most 2 rows name the same one
- question_length: int32 [64], P(('groups', 'enc', 'req')), parts along dimension 0, may hold values from 8 to 32
- question_embed: bfloat16 [4096, 8192], P(('groups', 'enc', 'req'), 'tensor'), parts along dimension 0, may hold values from -6 to 6
- enc_up: bfloat16 [1024, 4096], P(None, 'tensor'), may hold values from -0.1875 to 0.1875
- enc_down: bfloat16 [4096, 1024], P('tensor'), may hold values from -0.09375 to 0.09375
- enc_gain: float32 [1024], replicated, may hold values from 0.1 to 1.9
- proj_weight: bfloat16 [1024, 8192], P(None, 'tensor'), may hold values from -0.75 to 0.75
- norm_gain: float32 [8192], replicated, may hold values from 0.1 to 1.9
- q_weight: bfloat16 [8192, 4096], P(None, 'tensor'), may hold values from -2 to 2
- k_weight: bfloat16 [8192, 512], P(None, 'tensor'), may hold values from -1 to 1
- v_weight: bfloat16 [8192, 512], P(None, 'tensor'), may hold values from -0.0625 to 0.0625
- o_weight: bfloat16 [4096, 8192], P(None, 'tensor'), may hold values from -0.375 to 0.375
Outputs:
- layer_out: bfloat16 [4096, 8192], P(('groups', 'enc', 'req'), 'tensor'), parts along dimension 0
The draws below stay inside these ranges and needn't reach their ends.
There are 2 independent parts, one for each index of `groups`. The reference program is written for one: setup_inputs(seed, part) draws one part's arguments, and reference() takes and returns one part's arrays. A program takes and returns all parts, laid end to end along the dimension named above; an argument that names none is the same for every part. Nothing has to cross between parts.
Inputs may be any that keep to these rules, and one draw needn't show every extreme that they name: Span c belongs to request span_request[c, 0]; among the 64 spans of each aligned block of rows at most 2 belong to one request, and some block holds exactly 2 of one request. Every request has at least one span.
All inputs are finite; a program needn't handle non-finite values.
Results may differ from the reference program's by a relative error of at most 0.014.
Values may be sent and summed in bfloat16 or wider, within the bound.
A program may use at most 192 MiB of HBM per device.

```python
import math
import jax
import jax.numpy as jnp
import numpy as np
from jax import lax

D = 8192
HQ = 32
KVH = 4
HD = 128
D_E = 1024
FF_E = 4096
SPAN_LEN = 16
SLOT = 64
CAPR = 2
CH_DEV = 64
TOKENS = 2048
REQUESTS = 32
SPANS = 256
ENC_TOK = 4096


def shared_basis(key):
    return jax.random.normal(key, (D, KVH * HD), jnp.float32)


def draw_k_weight(key, part):
    basis = shared_basis(key)
    return jnp.clip(basis * D ** (-0.5), -1.0, 1.0).astype(jnp.bfloat16)


def draw_q_weight(key, part):
    key = jax.random.fold_in(key, 11)
    own_key = jax.random.fold_in(key, 0)
    noise = jax.random.normal(own_key, (D, HQ, HD), jnp.float32)
    return jnp.clip(noise * D ** (-0.5), -2.0, 2.0).reshape(D, HQ * HD).astype(jnp.bfloat16)


def with_ends(drawn, stream_key, low, largest):
    extent = drawn.shape
    place = [jax.random.randint(jax.random.fold_in(stream_key, axis), (), 0, extent[axis]) for axis in range(len(extent))]
    drawn = drawn.at[tuple(place)].set(low)
    longest = extent.index(max(extent))
    place[longest] = (place[longest] + 1) % extent[longest]
    return drawn.at[tuple(place)].set(largest)


def level_of(key, extent, cuts, least, high):
    def one(position, blocks):
        draws = jax.random.uniform(jax.random.fold_in(jax.random.fold_in(key, 6), position), (blocks,), jnp.float32, least / len(cuts), high / len(cuts))
        return jnp.repeat(jnp.exp(draws), extent[position] // blocks).reshape((-1,) + (1,) * (len(extent) - position - 1))

    factor_of = one(*cuts[0])
    for cut in cuts[1:]:
        factor_of = factor_of * one(*cut)
    return factor_of


def deal_out(key, own, number, rows, amount, top, most, skew):
    ranking = jax.random.permutation(key, amount)
    heavy_load, usual = load_shares(amount, rows * top, most, skew, True), load_shares(amount, rows * top, most, skew, False)
    places = jnp.arange(amount)

    def named(lengths, turn):
        used = int((lengths > 0).sum())
        fixed = max(1, used // 4)
        passed = fixed + (places - fixed + turn * (used - fixed)) % max(1, amount - fixed)
        return jnp.zeros((amount,), jnp.int32).at[ranking[jnp.where(places < fixed, places, passed)]].set(jnp.asarray(lengths, jnp.int32))

    lengths = jnp.where(number % 4 == 0, named(heavy_load, number // 4), named(usual, number - number // 4 - 1))
    mixed = jax.random.permutation(jax.random.fold_in(own, 3), amount)
    donor, sink = mixed[0:amount // 2 * 2:2], mixed[1:amount // 2 * 2:2]
    margin = jnp.minimum(lengths[donor] - 1, most - lengths[sink]) // 2
    margin = jnp.where((donor == ranking[0]) | (sink == ranking[0]) | (lengths[sink] == 0), 0, jnp.maximum(margin, 0))
    passed = jax.random.randint(jax.random.fold_in(own, 4), (amount // 2,), 0, 1 << 20) % (margin + 1)
    lengths = lengths.at[donor].add(-passed).at[sink].add(passed)
    items = jnp.searchsorted(jnp.cumsum(lengths), jnp.arange(rows * top), side="right").astype(jnp.int32)
    table = items.reshape(top, rows).T
    table = table[jax.random.permutation(jax.random.fold_in(own, 1), rows)]
    turn = jax.random.randint(jax.random.fold_in(own, 2), (rows, 1), 0, top)
    return jnp.take_along_axis(table, (jnp.arange(top)[None, :] + turn) % top, axis=1)


def load_shares(count, total, limit, lean, full):
    weights = [(1 << 20) // math.isqrt(rank ** lean) + 1 for rank in range(1, count + 1)]
    largest = limit if full else min(limit, max(-(-total // count), total * weights[0] // sum(weights)))
    least = 1 if total - largest >= count - 1 else 0
    holding, spare = [largest] + [least] * (count - 1), total - largest - least * (count - 1)
    while spare > 0:
        movable = [i for i in range(1, count) if holding[i] < largest] or [i for i in range(1, count) if holding[i] < limit]
        pool, budget = sum([weights[i] for i in movable]), spare
        for i in movable:
            addition = min(limit - holding[i], max(1, budget * weights[i] // pool), spare)
            holding[i] = holding[i] + addition
            spare = spare - addition
    return np.array(holding)


def gaussian(rng, extent, deviation, bound, cuts=(), held_as=jnp.bfloat16):
    entries = deviation * jax.random.normal(rng, extent, jnp.float32)
    if cuts:
        entries = entries * level_of(rng, extent, cuts, -0.22, 0.18)
    return jnp.clip(entries, -bound, bound).astype(held_as)


def setup_inputs(seed: int = 0, part: int = 0) -> dict:
    splits = jax.random.split(jax.random.key(seed), 14)
    own_keys = jax.random.split(jax.random.fold_in(splits[13], part), 14)
    span_tokens = gaussian(own_keys[0], (ENC_TOK, D_E), 1.0, 6.0, ((0, 4),))
    span_request_keys = jax.random.split(jax.random.fold_in(own_keys[1], 1), SPANS // CH_DEV)
    span_request_turns = jax.random.permutation(jax.random.fold_in(own_keys[1], 3), SPANS // CH_DEV)
    span_request = jax.vmap(lambda own, number: deal_out(jax.random.fold_in(own_keys[1], 2), own, number, CH_DEV, REQUESTS, 1, CAPR, 2))(span_request_keys, span_request_turns).reshape((SPANS, 1))
    question_length = with_ends(jax.random.randint(own_keys[2], (REQUESTS,), SLOT // 8, SLOT // 2 + 1), jax.random.fold_in(own_keys[2], 1), SLOT // 8, (SLOT // 2 + 1) - 1).astype(jnp.int32)
    question_embed = gaussian(own_keys[3], (TOKENS, D), 1.0, 6.0, ((0, 4), (1, 4)))
    enc_up = gaussian(splits[4], (D_E, FF_E), D_E ** -0.5, 0.1875, ((1, 4),))
    enc_down = gaussian(splits[5], (FF_E, D_E), FF_E ** -0.5, 0.09375, ((0, 4),))
    enc_gain = jnp.clip(1.0 + 0.18 * jax.random.normal(splits[6], (D_E,), jnp.float32), 0.1, 1.9)
    proj_weight = gaussian(splits[7], (D_E, D), (D_E // 16) ** -0.5, 0.75, ((1, 4),))
    norm_gain = jnp.clip(1.0 + 0.18 * jax.random.normal(splits[8], (D,), jnp.float32), 0.1, 1.9)
    q_weight = draw_q_weight(jax.random.fold_in(splits[13], 71), part)
    k_weight = draw_k_weight(jax.random.fold_in(splits[13], 71), part)
    v_weight = gaussian(splits[11], (D, KVH * HD), D ** -0.5, 0.0625, ((1, 4),))
    o_weight = gaussian(splits[12], (HQ * HD, D), (HQ * HD // 16) ** -0.5, 0.375, ((1, 4),))
    return {"span_tokens": span_tokens, "span_request": span_request, "question_length": question_length, "question_embed": question_embed, "enc_up": enc_up, "enc_down": enc_down, "enc_gain": enc_gain, "proj_weight": proj_weight, "norm_gain": norm_gain, "q_weight": q_weight, "k_weight": k_weight, "v_weight": v_weight, "o_weight": o_weight}


def rotate(values, positions):
    half_dim = values.shape[-1] // 2
    frequency = jnp.exp(jnp.arange(half_dim, dtype=jnp.float32) * (-2.0 * math.log(10000.0) / values.shape[-1]))
    angles = positions.astype(jnp.float32)[:, None] * frequency[None, :]
    cosine = jnp.cos(angles)[:, None, :]
    sines = jnp.sin(angles)[:, None, :]
    lower_half = values[..., :half_dim]
    upper_half = values[..., half_dim:]
    return jnp.concatenate([lower_half * cosine - upper_half * sines, upper_half * cosine + lower_half * sines], axis=-1)

def layer_norm(inputs, gain):
    center = inputs - lax.optimization_barrier(jnp.mean(inputs, axis=-1, keepdims=True))
    spread = lax.optimization_barrier(jnp.mean(center * center, axis=-1, keepdims=True))
    return center * lax.rsqrt(spread + 1e-05) * gain

def reference(span_tokens, span_request, question_length, question_embed, enc_up, enc_down, enc_gain, proj_weight, norm_gain, q_weight, k_weight, v_weight, o_weight):
    enc_hidden = jax.nn.gelu(jnp.dot(span_tokens, enc_up, preferred_element_type=jnp.float32), approximate=False).astype(jnp.bfloat16)
    enc_ffn = jnp.dot(enc_hidden, enc_down, preferred_element_type=jnp.float32)
    encoded = layer_norm(span_tokens.astype(jnp.float32) + enc_ffn, enc_gain)
    pooled = lax.optimization_barrier(jnp.mean(encoded.reshape(SPANS, SPAN_LEN, D_E), axis=1)).astype(jnp.bfloat16)
    span_embed = jnp.dot(pooled, proj_weight, preferred_element_type=jnp.float32).astype(jnp.bfloat16)
    owners_of = span_request[:, 0]
    member = (owners_of[None, :] == jnp.arange(REQUESTS, dtype=jnp.int32)[:, None]).astype(jnp.int32)
    before = jnp.cumsum(member, axis=1) - member
    arrive = lax.optimization_barrier(jnp.sum(before * member, axis=0))
    counts = lax.optimization_barrier(jnp.sum(member, axis=1))
    target = (owners_of * SLOT + arrive).astype(jnp.int32)
    span_rows = jnp.zeros((TOKENS, D), jnp.bfloat16).at[target].set(span_embed)
    positions = jnp.arange(SLOT, dtype=jnp.int32)
    is_span = positions[None, :] < counts[:, None]
    live = positions[None, :] < (counts + question_length)[:, None]
    is_question = jnp.logical_and(jnp.logical_not(is_span), live)
    question_rows = jnp.arange(REQUESTS, dtype=jnp.int32)[:, None] * SLOT + jnp.clip(positions[None, :] - counts[:, None], 0, SLOT - 1)
    from_questions = jnp.take(question_embed, question_rows.reshape(-1).astype(jnp.int32), axis=0)
    zero_rows = jnp.zeros_like(span_rows)
    decoder_in = jnp.where(is_span.reshape(-1, 1), span_rows, jnp.where(is_question.reshape(-1, 1), from_questions, zero_rows))
    inputs32 = decoder_in.astype(jnp.float32)
    normed = (inputs32 * lax.rsqrt(lax.optimization_barrier(jnp.mean(inputs32 * inputs32, axis=-1, keepdims=True)) + 1e-05) * norm_gain).astype(jnp.bfloat16)
    query_raw = jnp.dot(normed, q_weight, preferred_element_type=jnp.float32).reshape(REQUESTS, SLOT, HQ, HD)
    queries = rotate(query_raw, positions).astype(jnp.bfloat16)
    keys_raw = jnp.dot(normed, k_weight, preferred_element_type=jnp.float32).astype(jnp.bfloat16)
    values = jnp.dot(normed, v_weight, preferred_element_type=jnp.float32).astype(jnp.bfloat16)
    keys_heads = jnp.swapaxes(keys_raw.astype(jnp.float32).reshape(REQUESTS, SLOT, HD, KVH), 2, 3)
    keys = rotate(keys_heads, positions).astype(jnp.bfloat16)
    values = jnp.swapaxes(values.reshape(REQUESTS, SLOT, HD, KVH), 2, 3)
    head_map = jnp.arange(HQ, dtype=jnp.int32) // (HQ // KVH)
    keys_wide = keys[:, :, head_map, :]
    values_wide = values[:, :, head_map, :]
    scores = jnp.einsum('rphd,rqhd->rhpq', queries.astype(jnp.float32), keys_wide.astype(jnp.float32)) * HD ** (-0.5)
    allowed = jnp.logical_and((positions[:, None] >= positions[None, :])[None, None, :, :], live[:, None, None, :])
    scores = jnp.where(allowed, scores, -jnp.inf)
    probs = jax.nn.softmax(scores, axis=-1).astype(jnp.bfloat16)
    context = jnp.einsum('rhpq,rqhd->rphd', probs.astype(jnp.float32), values_wide.astype(jnp.float32)).astype(jnp.bfloat16)
    context = context.reshape(TOKENS, HQ * HD)
    summed = inputs32 + jnp.dot(context, o_weight, preferred_element_type=jnp.float32)
    return jnp.where(live.reshape(-1, 1), summed, jnp.zeros_like(summed)).astype(jnp.bfloat16)
```

```python
import math

import jax
import jax.numpy as jnp
from jax import lax
from jax.sharding import PartitionSpec as P

HQ = 32
KVH = 4
HD = 128
SPAN_LEN = 16
SLOT = 64
CAPR = 2
QUESTION_MAX = 32


def rope_tables(positions):
    half_dim = HD // 2
    frequency = jnp.exp(
        jnp.arange(half_dim, dtype=jnp.float32) * (-2.0 * math.log(10000.0) / HD)
    )
    angles = positions.astype(jnp.float32)[..., None] * frequency
    return jnp.cos(angles), jnp.sin(angles)


def rotate(values, cosine, sines):
    half_dim = values.shape[-1] // 2
    lower_half = values[..., :half_dim]
    upper_half = values[..., half_dim:]
    return jnp.concatenate(
        [lower_half * cosine - upper_half * sines, upper_half * cosine + lower_half * sines],
        axis=-1,
    )


def layer_norm(inputs, gain):
    center = inputs - jnp.mean(inputs, axis=-1, keepdims=True)
    spread = jnp.mean(center * center, axis=-1, keepdims=True)
    return center * lax.rsqrt(spread + 1e-05) * gain


def ffn_term(token_rows, enc_up, enc_down):
    enc_hidden = jax.nn.gelu(
        jnp.dot(token_rows, enc_up, preferred_element_type=jnp.float32), approximate=False
    ).astype(jnp.bfloat16)
    return jnp.dot(enc_hidden, enc_down, preferred_element_type=jnp.float32)


def pool_rows(token_rows, summed, enc_gain):
    encoded = layer_norm(token_rows.astype(jnp.float32) + summed, enc_gain)
    return jnp.mean(encoded.reshape(-1, SPAN_LEN, encoded.shape[-1]), axis=1).astype(jnp.bfloat16)


def rms(rows, gain):
    wide = rows.astype(jnp.float32)
    return (
        wide * lax.rsqrt(jnp.mean(wide * wide, axis=-1, keepdims=True) + 1e-05) * gain
    ).astype(jnp.bfloat16)


def shards(
    span_tokens,
    span_request,
    question_length,
    question_embed,
    enc_up,
    enc_down,
    enc_gain,
    proj_weight,
    norm_gain,
    q_weight,
    k_weight,
    v_weight,
    o_weight,
):
    tensor_count = lax.axis_size("tensor")
    tensor_place = lax.axis_index("tensor")
    owner_count = lax.axis_size(("enc", "req"))
    owner_place = lax.axis_index(("enc", "req"))
    requests_here = question_length.shape[0]
    columns = question_embed.shape[1]
    span_room = CAPR * owner_count
    room = min(SLOT, span_room + QUESTION_MAX)

    questions = question_embed.reshape(requests_here, SLOT, columns)[:, :QUESTION_MAX]
    questions = questions.reshape(-1, columns)
    question_full = lax.all_gather(questions, "tensor", axis=1, tiled=True)

    share_rows = span_tokens.shape[0] // tensor_count
    kept_sums = lax.psum_scatter(
        ffn_term(span_tokens, enc_up, enc_down).astype(jnp.bfloat16),
        "tensor",
        scatter_dimension=0,
        tiled=True,
    ).astype(jnp.float32)
    kept_tokens = lax.dynamic_slice_in_dim(span_tokens, tensor_place * share_rows, share_rows, 0)
    pooled = lax.all_gather(
        pool_rows(kept_tokens, kept_sums, enc_gain), "tensor", axis=0, tiled=True
    )

    spans_here = pooled.shape[0]
    owners_of = span_request[:, 0]
    all_spans = owners_of.shape[0]
    blocks = owners_of.reshape(owner_count, spans_here)
    index_here = jnp.arange(spans_here, dtype=jnp.int32)
    earlier = index_here[None, :] < index_here[:, None]
    my_spans = lax.dynamic_slice_in_dim(blocks, owner_place, 1, 0)[0]
    same_request = my_spans[None, :] == my_spans[:, None]
    rank_here = jnp.sum(jnp.logical_and(same_request, earlier).astype(jnp.int32), axis=1)
    slot_count = requests_here * CAPR
    placement = my_spans * CAPR + rank_here
    spot_index = jnp.arange(owner_count * slot_count, dtype=jnp.int32)
    selector = (spot_index[:, None] == placement[None, :]).astype(jnp.bfloat16)
    placed = jnp.dot(selector, pooled, preferred_element_type=jnp.float32).astype(jnp.bfloat16)
    incoming = lax.all_to_all(
        placed.reshape(owner_count, slot_count, -1),
        ("enc", "req"),
        split_axis=0,
        concat_axis=0,
        tiled=True,
    )
    incoming = incoming.reshape(owner_count, requests_here, CAPR, -1)
    incoming = jnp.swapaxes(incoming, 0, 1).reshape(requests_here * span_room, -1)
    span_rows = jnp.dot(incoming, proj_weight, preferred_element_type=jnp.float32).astype(
        jnp.bfloat16
    )
    span_full = lax.all_gather(span_rows, "tensor", axis=1, tiled=True)

    requests_all = requests_here * owner_count
    exact = all_spans == requests_all * span_room
    local_requests = owner_place * requests_here + jnp.arange(requests_here, dtype=jnp.int32)
    if exact:
        slot_positions = jnp.broadcast_to(
            jnp.arange(room, dtype=jnp.int32)[None, :], (requests_here, room)
        )
        counts = jnp.full((requests_here,), span_room, jnp.int32)
        live = slot_positions < (counts + question_length)[:, None]
    else:
        per_block = jnp.sum(
            (blocks[None, :, :] == local_requests[:, None, None]).astype(jnp.int32), axis=2
        )
        counts = jnp.sum(per_block, axis=1)
        before = jnp.cumsum(per_block, axis=1) - per_block
        rank = jnp.arange(CAPR, dtype=jnp.int32)
        span_positions = (before[:, :, None] + rank[None, None, :]).reshape(requests_here, -1)
        span_live = (rank[None, None, :] < per_block[:, :, None]).reshape(requests_here, -1)
        turn = jnp.arange(QUESTION_MAX, dtype=jnp.int32)
        question_positions = counts[:, None] + turn[None, :]
        question_live = turn[None, :] < question_length[:, None]
        slot_positions = jnp.concatenate([span_positions, question_positions], axis=1)
        live = jnp.concatenate([span_live, question_live], axis=1)

    kv_columns = k_weight.shape[1]
    entries = kv_columns // KVH
    kv_weight = jnp.stack(
        [k_weight.reshape(-1, entries, KVH), v_weight.reshape(-1, entries, KVH)], axis=1
    )
    kv_weight = jnp.transpose(kv_weight, (0, 3, 1, 2)).reshape(k_weight.shape[0], -1)
    heads_here = q_weight.shape[1] // HD

    def project(rows, slots):
        normed = rms(rows, norm_gain)
        kv = jnp.dot(normed, kv_weight, preferred_element_type=jnp.float32).astype(jnp.bfloat16)
        query = jnp.dot(normed, q_weight, preferred_element_type=jnp.float32)
        cosine, sines = rope_tables(slots)
        query = rotate(
            query.reshape(requests_here, -1, heads_here, HD),
            cosine[:, :, None, :],
            sines[:, :, None, :],
        ).astype(jnp.bfloat16)
        return query, kv.reshape(requests_here, -1, 2 * kv_columns)

    question_queries, question_kv = project(question_full, slot_positions[:, span_room:])
    span_queries, span_kv = project(span_full, slot_positions[:, :span_room])
    queries = jnp.concatenate([span_queries, question_queries], axis=1)
    kv = jnp.concatenate([span_kv, question_kv], axis=1)
    slots = kv.shape[1]
    if tensor_count == KVH:
        kv = kv.reshape(requests_here * slots, KVH, 2 * entries)
        kv = lax.all_to_all(
            jnp.swapaxes(kv, 0, 1), "tensor", split_axis=0, concat_axis=0, tiled=True
        )
        kv = kv.reshape(tensor_count, requests_here, slots, 2, entries)
    else:
        kv = lax.all_gather(kv, "tensor", axis=0, tiled=False)
        kv = kv.reshape(tensor_count, requests_here, slots, KVH, 2, entries)
        shared_head = tensor_place * heads_here // (HQ // KVH)
        kv = lax.dynamic_slice_in_dim(kv, shared_head, 1, 3)[:, :, :, 0]
    kv = jnp.transpose(kv, (3, 1, 2, 0, 4)).reshape(2, requests_here, slots, HD)
    cosine, sines = rope_tables(slot_positions)
    keys = rotate(kv[0].astype(jnp.float32), cosine, sines).astype(jnp.bfloat16)
    values = kv[1]

    local_rows = jnp.concatenate(
        [
            span_rows.reshape(requests_here, span_room, columns),
            questions.reshape(requests_here, QUESTION_MAX, columns),
        ],
        axis=1,
    )
    if not exact:
        at = jnp.arange(room, dtype=jnp.int32)
        order = jnp.logical_and(
            at[None, :, None] == slot_positions[:, None, :], live[:, None, :]
        ).astype(jnp.bfloat16)
        local_rows = jnp.einsum(
            "rps,rsc->rpc", order, local_rows, preferred_element_type=jnp.float32
        ).astype(jnp.bfloat16)
    live_rows = jnp.arange(room, dtype=jnp.int32)[None, :] < (counts + question_length)[:, None]

    def attend(low, high):
        scores = jnp.einsum(
            "rphd,rqd->rhpq",
            queries[low:high],
            keys[low:high],
            preferred_element_type=jnp.float32,
        ) * HD ** (-0.5)
        spots = slot_positions[low:high]
        allowed = jnp.logical_and(
            spots[:, :, None] >= spots[:, None, :], live[low:high][:, None, :]
        )
        scores = jnp.where(allowed[:, None], scores, -1e30)
        probs = jax.nn.softmax(scores, axis=-1).astype(jnp.bfloat16)
        context = jnp.einsum(
            "rhpq,rqd->rphd", probs, values[low:high], preferred_element_type=jnp.float32
        ).astype(jnp.bfloat16)
        context = context.reshape(high - low, slots, heads_here * HD)
        if not exact:
            context = jnp.einsum(
                "rps,rsc->rpc", order[low:high], context, preferred_element_type=jnp.float32
            ).astype(jnp.bfloat16)
        return lax.all_gather(
            context.reshape((high - low) * room, -1), "tensor", axis=1, tiled=True
        )

    half = requests_here // 2
    outs = []
    for low, high in ((0, half), (half, requests_here)):
        mixed = jnp.dot(attend(low, high), o_weight, preferred_element_type=jnp.float32)
        mixed = mixed.reshape(high - low, room, columns)
        summed = local_rows[low:high].astype(jnp.float32) + mixed
        outs.append(
            jnp.where(live_rows[low:high][:, :, None], summed, jnp.zeros_like(summed)).astype(
                jnp.bfloat16
            )
        )
    out = jnp.concatenate(outs, axis=0)
    return jnp.pad(out, ((0, 0), (0, SLOT - room), (0, 0))).reshape(-1, columns)


def solution(mesh):
    return jax.shard_map(
        shards,
        mesh=mesh,
        in_specs=(
            P(("groups", "enc", "req"), None),
            P("groups", None),
            P(("groups", "enc", "req")),
            P(("groups", "enc", "req"), "tensor"),
            P(None, "tensor"),
            P("tensor", None),
            P(),
            P(None, "tensor"),
            P(),
            P(None, "tensor"),
            P(None, "tensor"),
            P(None, "tensor"),
            P(None, "tensor"),
        ),
        out_specs=P(("groups", "enc", "req"), "tensor"),
        check_vma=False,
    )
```

```python
import functools
import math

import jax
import jax.numpy as jnp
from jax import lax
from jax.experimental import pallas as pl
from jax.experimental.pallas import tpu as pltpu
from jax.sharding import PartitionSpec as P

HQ = 32
KVH = 4
HD = 128
SPAN_LEN = 16
SLOT = 64
CAPR = 2
QUESTION_MAX = 32


def rope_tables(positions):
    half_dim = HD // 2
    frequency = jnp.exp(
        jnp.arange(half_dim, dtype=jnp.float32) * (-2.0 * math.log(10000.0) / HD)
    )
    angles = positions.astype(jnp.float32)[..., None] * frequency
    return jnp.cos(angles), jnp.sin(angles)


def rotate(values, cosine, sines):
    half_dim = values.shape[-1] // 2
    lower_half = values[..., :half_dim]
    upper_half = values[..., half_dim:]
    return jnp.concatenate(
        [lower_half * cosine - upper_half * sines, upper_half * cosine + lower_half * sines],
        axis=-1,
    )


def copy_to(src, dst, send_sem, recv_sem, target):
    return pltpu.make_async_remote_copy(
        src_ref=src,
        dst_ref=dst,
        send_sem=send_sem,
        recv_sem=recv_sem,
        device_id=target,
        device_id_type=pl.DeviceIdType.MESH,
    )


def front_kernel(
    n,
    enc_n,
    req_n,
    tokens,
    enc_up,
    enc_down,
    enc_gain,
    proj_weight,
    selector,
    reorder,
    question_rows,
    question_full,
    span_full,
    partial_out,
    partial_in,
    own_sum,
    pooled,
    placed,
    incoming,
    own_sem,
    right_send,
    right_recv,
    left_send,
    left_recv,
    sum_send,
    sum_recv,
    pool_send,
    pool_recv,
    owner_send,
    owner_recv,
    span_send,
    span_recv,
):
    owners = enc_n * req_n
    me = lax.axis_index("tensor")
    my_owner = lax.axis_index("enc") * req_n + lax.axis_index("req")
    share = own_sum.shape[0]

    def tensor_peer(distance):
        return {"tensor": lax.rem(me + distance, n)}

    def owner_peer(distance):
        other = lax.rem(my_owner + distance, owners)
        return other, {"enc": other // req_n, "req": lax.rem(other, req_n)}

    barrier = pltpu.get_barrier_semaphore()
    for distance in range(1, n):
        pl.semaphore_signal(
            barrier,
            inc=1,
            device_id=tensor_peer(distance),
            device_id_type=pl.DeviceIdType.MESH,
        )
    for distance in range(1, owners):
        pl.semaphore_signal(
            barrier,
            inc=1,
            device_id=owner_peer(distance)[1],
            device_id_type=pl.DeviceIdType.MESH,
        )
    pl.semaphore_wait(barrier, n - 1 + owners - 1)

    own_rows = question_rows.at[:, :QUESTION_MAX]
    own_copy = pltpu.make_async_copy(own_rows, question_full.at[me], own_sem)
    own_copy.start()

    def rightward(step):
        block = jnp.maximum(me - step, 0)
        source = own_rows if step == 0 else question_full.at[block]
        copy = copy_to(
            source,
            question_full.at[block],
            right_send.at[step],
            right_recv.at[step],
            {"tensor": jnp.minimum(me + 1, n - 1)},
        )
        return copy, jnp.logical_and(me - step >= 0, me + 1 < n)

    def leftward(step):
        block = jnp.minimum(me + step, n - 1)
        source = own_rows if step == 0 else question_full.at[block]
        copy = copy_to(
            source,
            question_full.at[block],
            left_send.at[step],
            left_recv.at[step],
            {"tensor": jnp.maximum(me - 1, 0)},
        )
        return copy, jnp.logical_and(me + step < n, me >= 1)

    def send_step(step):
        for copy, valid in (rightward(step), leftward(step)):
            pl.when(valid)(copy.start)

    def arrive_step(step):
        @pl.when(me - 1 - step >= 0)
        def _():
            block = jnp.maximum(me - 1 - step, 0)
            copy_to(
                own_rows,
                question_full.at[block],
                right_send.at[step],
                right_recv.at[step],
                {"tensor": jnp.minimum(me + 1, n - 1)},
            ).wait_recv()

        @pl.when(me + 1 + step < n)
        def _():
            block = jnp.minimum(me + 1 + step, n - 1)
            copy_to(
                own_rows,
                question_full.at[block],
                left_send.at[step],
                left_recv.at[step],
                {"tensor": jnp.maximum(me - 1, 0)},
            ).wait_recv()

    send_step(0)

    def term(place):
        rows = tokens[pl.ds(pl.multiple_of(place * share, share), share), :]
        hidden = jnp.dot(rows, enc_up[...], preferred_element_type=jnp.float32)
        hidden = 0.5 * hidden * (1.0 + lax.erf(hidden * math.sqrt(0.5)))
        return jnp.dot(
            hidden.astype(jnp.bfloat16), enc_down[...], preferred_element_type=jnp.float32
        )

    def sum_copy(slot):
        return copy_to(
            partial_out.at[slot],
            partial_in.at[slot],
            sum_send.at[slot],
            sum_recv.at[slot],
            tensor_peer(slot + 1),
        )

    @pl.loop(0, n - 1)
    def _(slot):
        partial_out[slot] = term(lax.rem(me + slot + 1, n)).astype(jnp.bfloat16)
        sum_copy(slot).start()

    own_tokens = tokens[pl.ds(pl.multiple_of(me * share, share), share), :]
    own_sum[...] = term(me) + own_tokens.astype(jnp.float32)

    if n > 2:
        arrive_step(0)
        send_step(1)

    for slot in range(n - 1):
        sum_copy(slot).wait_recv()
        own_sum[...] += partial_in[slot].astype(jnp.float32)
    summed = own_sum[...]
    center = summed - jnp.mean(summed, axis=-1, keepdims=True)
    spread = jnp.mean(center * center, axis=-1, keepdims=True)
    encoded = center * lax.rsqrt(spread + 1e-05) * enc_gain[...]
    pooled[me] = jnp.mean(
        encoded.reshape(share // SPAN_LEN, SPAN_LEN, encoded.shape[-1]), axis=1
    ).astype(jnp.bfloat16)

    def pool_copy(slot):
        return copy_to(
            pooled.at[me],
            pooled.at[me],
            pool_send.at[slot],
            pool_recv.at[slot],
            tensor_peer(slot + 1),
        )

    for slot in range(n - 1):
        pool_copy(slot).start()
    for slot in range(n - 1):
        source = lax.rem(me + n - 1 - slot, n)
        copy_to(
            pooled.at[source],
            pooled.at[source],
            pool_send.at[slot],
            pool_recv.at[slot],
            tensor_peer(slot + 1),
        ).wait_recv()

    for owner in range(owners):
        total = jnp.zeros(placed.shape[1:], jnp.float32)
        for place in range(n):
            total += jnp.dot(
                selector[owner, place], pooled[place], preferred_element_type=jnp.float32
            )
        placed[owner] = total.astype(jnp.bfloat16)
    incoming[my_owner] = placed[my_owner]

    def owner_copy(slot):
        other, target = owner_peer(slot + 1)
        return copy_to(
            placed.at[other],
            incoming.at[my_owner],
            owner_send.at[slot],
            owner_recv.at[slot],
            target,
        )

    for slot in range(owners - 1):
        owner_copy(slot).start()
    for slot in range(owners - 1):
        source = lax.rem(my_owner + owners - 1 - slot, owners)
        copy_to(
            placed.at[source],
            incoming.at[source],
            owner_send.at[slot],
            owner_recv.at[slot],
            owner_peer(slot + 1)[1],
        ).wait_recv()

    ordered = jnp.zeros((span_full.shape[1], incoming.shape[2]), jnp.float32)
    for owner in range(owners):
        ordered += jnp.dot(
            reorder[owner], incoming[owner], preferred_element_type=jnp.float32
        )
    span_full[me] = jnp.dot(
        ordered.astype(jnp.bfloat16), proj_weight[...], preferred_element_type=jnp.float32
    ).astype(jnp.bfloat16)

    def span_copy(slot):
        return copy_to(
            span_full.at[me],
            span_full.at[me],
            span_send.at[slot],
            span_recv.at[slot],
            tensor_peer(slot + 1),
        )

    for slot in range(n - 1):
        span_copy(slot).start()

    for step in range(2, n - 1):
        arrive_step(step - 1)
        send_step(step)
    arrive_step(n - 2)

    for slot in range(n - 1):
        source = lax.rem(me + n - 1 - slot, n)
        copy_to(
            span_full.at[source],
            span_full.at[source],
            span_send.at[slot],
            span_recv.at[slot],
            tensor_peer(slot + 1),
        ).wait_recv()

    own_copy.wait()
    for slot in range(n - 1):
        sum_copy(slot).wait_send()
        pool_copy(slot).wait_send()
        span_copy(slot).wait_send()
        for copy, valid in (rightward(slot), leftward(slot)):
            pl.when(valid)(copy.wait_send)
    for slot in range(owners - 1):
        owner_copy(slot).wait_send()


def front(
    n, enc_n, req_n, tokens, enc_up, enc_down, enc_gain, proj_weight, selector, reorder, rows
):
    owners = enc_n * req_n
    requests, _, columns = rows.shape
    share = tokens.shape[0] // n
    width = tokens.shape[1]
    slots = requests * CAPR
    vmem = pl.BlockSpec(memory_space=pltpu.VMEM)
    hbm = pl.BlockSpec(memory_space=pl.ANY)
    dma = pltpu.SemaphoreType.DMA
    return pl.pallas_call(
        functools.partial(front_kernel, n, enc_n, req_n),
        out_shape=(
            jax.ShapeDtypeStruct((n, requests, QUESTION_MAX, columns), jnp.bfloat16),
            jax.ShapeDtypeStruct((n, slots * owners, columns), jnp.bfloat16),
        ),
        in_specs=[vmem] * 7 + [hbm],
        out_specs=(hbm, vmem),
        scratch_shapes=[
            pltpu.VMEM((n - 1, share, width), jnp.bfloat16),
            pltpu.VMEM((n - 1, share, width), jnp.bfloat16),
            pltpu.VMEM((share, width), jnp.float32),
            pltpu.VMEM((n, share // SPAN_LEN, width), jnp.bfloat16),
            pltpu.VMEM((owners, slots, width), jnp.bfloat16),
            pltpu.VMEM((owners, slots, width), jnp.bfloat16),
            dma,
        ]
        + [dma((n - 1,))] * 8
        + [dma((owners - 1,))] * 2
        + [dma((n - 1,))] * 2,
        compiler_params=pltpu.CompilerParams(
            collective_id=0, has_side_effects=True, vmem_limit_bytes=40 * 1024 * 1024
        ),
        name="front",
    )(tokens, enc_up, enc_down, enc_gain.reshape(1, -1), proj_weight, selector, reorder, rows)


def rms(rows, gain):
    wide = rows.astype(jnp.float32)
    return (
        wide * lax.rsqrt(jnp.mean(wide * wide, axis=-1, keepdims=True) + 1e-05) * gain
    ).astype(jnp.bfloat16)


def shards(
    span_tokens,
    span_request,
    question_length,
    question_embed,
    enc_up,
    enc_down,
    enc_gain,
    proj_weight,
    norm_gain,
    q_weight,
    k_weight,
    v_weight,
    o_weight,
):
    tensor_count = lax.axis_size("tensor")
    tensor_place = lax.axis_index("tensor")
    owner_count = lax.axis_size(("enc", "req"))
    owner_place = lax.axis_index(("enc", "req"))
    requests_here = question_length.shape[0]
    columns = question_embed.shape[1]
    span_room = CAPR * owner_count
    room = min(SLOT, span_room + QUESTION_MAX)

    question_rows = question_embed.reshape(requests_here, SLOT, columns)
    questions = question_rows[:, :QUESTION_MAX].reshape(-1, columns)

    spans_here = span_tokens.shape[0] // SPAN_LEN
    owners_of = span_request[:, 0]
    all_spans = owners_of.shape[0]
    blocks = owners_of.reshape(owner_count, spans_here)
    index_here = jnp.arange(spans_here, dtype=jnp.int32)
    earlier = index_here[None, :] < index_here[:, None]
    my_spans = lax.dynamic_slice_in_dim(blocks, owner_place, 1, 0)[0]
    same_request = my_spans[None, :] == my_spans[:, None]
    rank_here = jnp.sum(jnp.logical_and(same_request, earlier).astype(jnp.int32), axis=1)
    slot_count = requests_here * CAPR
    placement = my_spans * CAPR + rank_here
    spot_index = jnp.arange(owner_count * slot_count, dtype=jnp.int32)
    selector = (spot_index[:, None] == placement[None, :]).astype(jnp.bfloat16)
    selector = selector.reshape(owner_count, slot_count, tensor_count, -1).swapaxes(1, 2)
    order = jnp.arange(owner_count * slot_count, dtype=jnp.int32)
    from_row = (
        order // CAPR % owner_count * slot_count + order // span_room * CAPR + order % CAPR
    )
    reorder = (from_row[None, :, None] == order.reshape(owner_count, 1, slot_count)).astype(
        jnp.bfloat16
    )
    question_full, span_full = front(
        tensor_count,
        lax.axis_size("enc"),
        lax.axis_size("req"),
        span_tokens,
        enc_up,
        enc_down,
        enc_gain,
        proj_weight,
        selector,
        reorder,
        question_rows,
    )
    span_rows = lax.dynamic_index_in_dim(span_full, tensor_place, 0, keepdims=False)
    question_full = question_full.reshape(tensor_count, -1, columns)
    question_full = jnp.swapaxes(question_full, 0, 1).reshape(-1, tensor_count * columns)
    span_full = jnp.swapaxes(span_full, 0, 1).reshape(-1, tensor_count * columns)

    requests_all = requests_here * owner_count
    exact = all_spans == requests_all * span_room
    local_requests = owner_place * requests_here + jnp.arange(requests_here, dtype=jnp.int32)
    if exact:
        slot_positions = jnp.broadcast_to(
            jnp.arange(room, dtype=jnp.int32)[None, :], (requests_here, room)
        )
        counts = jnp.full((requests_here,), span_room, jnp.int32)
        live = slot_positions < (counts + question_length)[:, None]
    else:
        per_block = jnp.sum(
            (blocks[None, :, :] == local_requests[:, None, None]).astype(jnp.int32), axis=2
        )
        counts = jnp.sum(per_block, axis=1)
        before = jnp.cumsum(per_block, axis=1) - per_block
        rank = jnp.arange(CAPR, dtype=jnp.int32)
        span_positions = (before[:, :, None] + rank[None, None, :]).reshape(requests_here, -1)
        span_live = (rank[None, None, :] < per_block[:, :, None]).reshape(requests_here, -1)
        turn = jnp.arange(QUESTION_MAX, dtype=jnp.int32)
        question_positions = counts[:, None] + turn[None, :]
        question_live = turn[None, :] < question_length[:, None]
        slot_positions = jnp.concatenate([span_positions, question_positions], axis=1)
        live = jnp.concatenate([span_live, question_live], axis=1)

    kv_columns = k_weight.shape[1]
    entries = kv_columns // KVH
    spot = jnp.arange(2 * kv_columns, dtype=jnp.int32)
    head_of, kind_of, entry_of = (
        spot // (2 * entries),
        spot // entries % 2,
        spot % entries,
    )
    regroup = (
        spot[:, None] == (kind_of * kv_columns + entry_of * KVH + head_of)[None, :]
    ).astype(jnp.bfloat16)
    heads_here = q_weight.shape[1] // HD

    def project(rows, slots):
        normed = rms(rows, norm_gain)
        kv = jnp.concatenate(
            [
                jnp.dot(normed, weight, preferred_element_type=jnp.float32).astype(jnp.bfloat16)
                for weight in (k_weight, v_weight)
            ],
            axis=1,
        )
        kv = jnp.dot(kv, regroup, preferred_element_type=jnp.float32).astype(jnp.bfloat16)
        query = jnp.dot(normed, q_weight, preferred_element_type=jnp.float32)
        cosine, sines = rope_tables(slots)
        query = rotate(
            query.reshape(requests_here, -1, heads_here, HD),
            cosine[:, :, None, :],
            sines[:, :, None, :],
        ).astype(jnp.bfloat16)
        return query, kv.reshape(requests_here, -1, 2 * kv_columns)

    question_queries, question_kv = project(question_full, slot_positions[:, span_room:])
    span_queries, span_kv = project(span_full, slot_positions[:, :span_room])
    queries = jnp.concatenate([span_queries, question_queries], axis=1)
    kv = jnp.concatenate([span_kv, question_kv], axis=1)
    slots = kv.shape[1]
    if tensor_count == KVH:
        kv = kv.reshape(requests_here * slots, KVH, 2 * entries)
        kv = lax.all_to_all(
            jnp.swapaxes(kv, 0, 1), "tensor", split_axis=0, concat_axis=0, tiled=True
        )
        kv = kv.reshape(tensor_count, requests_here, slots, 2, entries)
    else:
        kv = lax.all_gather(kv, "tensor", axis=0, tiled=False)
        kv = kv.reshape(tensor_count, requests_here, slots, KVH, 2, entries)
        shared_head = tensor_place * heads_here // (HQ // KVH)
        kv = lax.dynamic_slice_in_dim(kv, shared_head, 1, 3)[:, :, :, 0]
    kv = jnp.transpose(kv, (3, 1, 2, 0, 4)).reshape(2, requests_here, slots, HD)
    cosine, sines = rope_tables(slot_positions)
    keys = rotate(kv[0].astype(jnp.float32), cosine, sines).astype(jnp.bfloat16)
    values = kv[1]

    local_rows = jnp.concatenate(
        [
            span_rows.reshape(requests_here, span_room, columns),
            questions.reshape(requests_here, QUESTION_MAX, columns),
        ],
        axis=1,
    )
    if not exact:
        at = jnp.arange(room, dtype=jnp.int32)
        order = jnp.logical_and(
            at[None, :, None] == slot_positions[:, None, :], live[:, None, :]
        ).astype(jnp.bfloat16)
        local_rows = jnp.einsum(
            "rps,rsc->rpc", order, local_rows, preferred_element_type=jnp.float32
        ).astype(jnp.bfloat16)
    live_rows = jnp.arange(room, dtype=jnp.int32)[None, :] < (counts + question_length)[:, None]

    def attend(low, high):
        scores = jnp.einsum(
            "rphd,rqd->rhpq",
            queries[low:high],
            keys[low:high],
            preferred_element_type=jnp.float32,
        ) * HD ** (-0.5)
        spots = slot_positions[low:high]
        allowed = jnp.logical_and(
            spots[:, :, None] >= spots[:, None, :], live[low:high][:, None, :]
        )
        scores = jnp.where(allowed[:, None], scores, -1e30)
        probs = jax.nn.softmax(scores, axis=-1).astype(jnp.bfloat16)
        context = jnp.einsum(
            "rhpq,rqd->rphd", probs, values[low:high], preferred_element_type=jnp.float32
        ).astype(jnp.bfloat16)
        context = context.reshape(high - low, slots, heads_here * HD)
        if not exact:
            context = jnp.einsum(
                "rps,rsc->rpc", order[low:high], context, preferred_element_type=jnp.float32
            ).astype(jnp.bfloat16)
        return lax.all_gather(
            context.reshape((high - low) * room, -1), "tensor", axis=1, tiled=True
        )

    half = requests_here // 2
    outs = []
    for low, high in ((0, half), (half, requests_here)):
        mixed = jnp.dot(attend(low, high), o_weight, preferred_element_type=jnp.float32)
        mixed = mixed.reshape(high - low, room, columns)
        summed = local_rows[low:high].astype(jnp.float32) + mixed
        outs.append(
            jnp.where(live_rows[low:high][:, :, None], summed, jnp.zeros_like(summed)).astype(
                jnp.bfloat16
            )
        )
    out = jnp.concatenate(outs, axis=0)
    return jnp.pad(out, ((0, 0), (0, SLOT - room), (0, 0))).reshape(-1, columns)


def solution(mesh):
    return jax.shard_map(
        shards,
        mesh=mesh,
        in_specs=(
            P(("groups", "enc", "req"), None),
            P("groups", None),
            P(("groups", "enc", "req")),
            P(("groups", "enc", "req"), "tensor"),
            P(None, "tensor"),
            P("tensor", None),
            P(),
            P(None, "tensor"),
            P(),
            P(None, "tensor"),
            P(None, "tensor"),
            P(None, "tensor"),
            P(None, "tensor"),
        ),
        out_specs=P(("groups", "enc", "req"), "tensor"),
        check_vma=False,
    )
```

```python
import functools
import math

import jax
import jax.numpy as jnp
from jax import lax
from jax.experimental import pallas as pl
from jax.experimental.pallas import tpu as pltpu
from jax.sharding import PartitionSpec as P

HQ = 32
KVH = 4
HD = 128
SPAN_LEN = 16
SLOT = 64
CAPR = 2
QUESTION_MAX = 32


def rope_tables(positions):
    half_dim = HD // 2
    frequency = jnp.exp(
        jnp.arange(half_dim, dtype=jnp.float32) * (-2.0 * math.log(10000.0) / HD)
    )
    angles = positions.astype(jnp.float32)[..., None] * frequency
    return jnp.cos(angles), jnp.sin(angles)


def rotate(values, cosine, sines):
    half_dim = values.shape[-1] // 2
    lower_half = values[..., :half_dim]
    upper_half = values[..., half_dim:]
    return jnp.concatenate(
        [lower_half * cosine - upper_half * sines, upper_half * cosine + lower_half * sines],
        axis=-1,
    )


def copy_to(src, dst, send_sem, recv_sem, target):
    return pltpu.make_async_remote_copy(
        src_ref=src,
        dst_ref=dst,
        send_sem=send_sem,
        recv_sem=recv_sem,
        device_id=target,
        device_id_type=pl.DeviceIdType.MESH,
    )


def front_kernel(
    n,
    enc_n,
    req_n,
    tokens,
    enc_up,
    enc_down,
    enc_gain,
    proj_weight,
    selector,
    reorder,
    question_rows,
    question_full,
    span_full,
    partial_out,
    partial_in,
    own_sum,
    pooled,
    placed,
    incoming,
    own_sem,
    right_send,
    right_recv,
    left_send,
    left_recv,
    sum_send,
    sum_recv,
    pool_send,
    pool_recv,
    owner_send,
    owner_recv,
    span_send,
    span_recv,
):
    owners = enc_n * req_n
    me = lax.axis_index("tensor")
    my_owner = lax.axis_index("enc") * req_n + lax.axis_index("req")
    share = own_sum.shape[0]

    def tensor_peer(distance):
        return {"tensor": lax.rem(me + distance, n)}

    def owner_peer(distance):
        other = lax.rem(my_owner + distance, owners)
        return other, {"enc": other // req_n, "req": lax.rem(other, req_n)}

    barrier = pltpu.get_barrier_semaphore()
    for distance in range(1, n):
        pl.semaphore_signal(
            barrier,
            inc=1,
            device_id=tensor_peer(distance),
            device_id_type=pl.DeviceIdType.MESH,
        )
    for distance in range(1, owners):
        pl.semaphore_signal(
            barrier,
            inc=1,
            device_id=owner_peer(distance)[1],
            device_id_type=pl.DeviceIdType.MESH,
        )
    pl.semaphore_wait(barrier, n - 1 + owners - 1)

    own_rows = question_rows.at[:, :QUESTION_MAX]
    own_copy = pltpu.make_async_copy(own_rows, question_full.at[me], own_sem)
    own_copy.start()

    def rightward(step):
        block = jnp.maximum(me - step, 0)
        source = own_rows if step == 0 else question_full.at[block]
        copy = copy_to(
            source,
            question_full.at[block],
            right_send.at[step],
            right_recv.at[step],
            {"tensor": jnp.minimum(me + 1, n - 1)},
        )
        return copy, jnp.logical_and(me - step >= 0, me + 1 < n)

    def leftward(step):
        block = jnp.minimum(me + step, n - 1)
        source = own_rows if step == 0 else question_full.at[block]
        copy = copy_to(
            source,
            question_full.at[block],
            left_send.at[step],
            left_recv.at[step],
            {"tensor": jnp.maximum(me - 1, 0)},
        )
        return copy, jnp.logical_and(me + step < n, me >= 1)

    def send_step(step):
        for copy, valid in (rightward(step), leftward(step)):
            pl.when(valid)(copy.start)

    def arrive_step(step):
        @pl.when(me - 1 - step >= 0)
        def _():
            block = jnp.maximum(me - 1 - step, 0)
            copy_to(
                own_rows,
                question_full.at[block],
                right_send.at[step],
                right_recv.at[step],
                {"tensor": jnp.minimum(me + 1, n - 1)},
            ).wait_recv()

        @pl.when(me + 1 + step < n)
        def _():
            block = jnp.minimum(me + 1 + step, n - 1)
            copy_to(
                own_rows,
                question_full.at[block],
                left_send.at[step],
                left_recv.at[step],
                {"tensor": jnp.maximum(me - 1, 0)},
            ).wait_recv()

    send_step(0)

    def term(place):
        rows = tokens[pl.ds(pl.multiple_of(place * share, share), share), :]
        hidden = jnp.dot(rows, enc_up[...], preferred_element_type=jnp.float32)
        hidden = 0.5 * hidden * (1.0 + lax.erf(hidden * math.sqrt(0.5)))
        return jnp.dot(
            hidden.astype(jnp.bfloat16), enc_down[...], preferred_element_type=jnp.float32
        )

    def sum_copy(slot):
        return copy_to(
            partial_out.at[slot],
            partial_in.at[slot],
            sum_send.at[slot],
            sum_recv.at[slot],
            tensor_peer(slot + 1),
        )

    @pl.loop(0, n - 1)
    def _(slot):
        partial_out[slot] = term(lax.rem(me + slot + 1, n)).astype(jnp.bfloat16)
        sum_copy(slot).start()

    own_tokens = tokens[pl.ds(pl.multiple_of(me * share, share), share), :]
    own_sum[...] = term(me) + own_tokens.astype(jnp.float32)

    if n > 2:
        arrive_step(0)
        send_step(1)

    for slot in range(n - 1):
        sum_copy(slot).wait_recv()
        own_sum[...] += partial_in[slot].astype(jnp.float32)
    summed = own_sum[...]
    center = summed - jnp.mean(summed, axis=-1, keepdims=True)
    spread = jnp.mean(center * center, axis=-1, keepdims=True)
    encoded = center * lax.rsqrt(spread + 1e-05) * enc_gain[...]
    pooled[me] = jnp.mean(
        encoded.reshape(share // SPAN_LEN, SPAN_LEN, encoded.shape[-1]), axis=1
    ).astype(jnp.bfloat16)

    def pool_copy(slot):
        return copy_to(
            pooled.at[me],
            pooled.at[me],
            pool_send.at[slot],
            pool_recv.at[slot],
            tensor_peer(slot + 1),
        )

    for slot in range(n - 1):
        pool_copy(slot).start()
    for slot in range(n - 1):
        source = lax.rem(me + n - 1 - slot, n)
        copy_to(
            pooled.at[source],
            pooled.at[source],
            pool_send.at[slot],
            pool_recv.at[slot],
            tensor_peer(slot + 1),
        ).wait_recv()

    for owner in range(owners):
        total = jnp.zeros(placed.shape[1:], jnp.float32)
        for place in range(n):
            total += jnp.dot(
                selector[owner, place], pooled[place], preferred_element_type=jnp.float32
            )
        placed[owner] = total.astype(jnp.bfloat16)
    incoming[my_owner] = placed[my_owner]

    def owner_copy(slot):
        other, target = owner_peer(slot + 1)
        return copy_to(
            placed.at[other],
            incoming.at[my_owner],
            owner_send.at[slot],
            owner_recv.at[slot],
            target,
        )

    for slot in range(owners - 1):
        owner_copy(slot).start()
    for slot in range(owners - 1):
        source = lax.rem(my_owner + owners - 1 - slot, owners)
        copy_to(
            placed.at[source],
            incoming.at[source],
            owner_send.at[slot],
            owner_recv.at[slot],
            owner_peer(slot + 1)[1],
        ).wait_recv()

    ordered = jnp.zeros((span_full.shape[1], incoming.shape[2]), jnp.float32)
    for owner in range(owners):
        ordered += jnp.dot(
            reorder[owner], incoming[owner], preferred_element_type=jnp.float32
        )
    span_full[me] = jnp.dot(
        ordered.astype(jnp.bfloat16), proj_weight[...], preferred_element_type=jnp.float32
    ).astype(jnp.bfloat16)

    def span_copy(slot):
        return copy_to(
            span_full.at[me],
            span_full.at[me],
            span_send.at[slot],
            span_recv.at[slot],
            tensor_peer(slot + 1),
        )

    for slot in range(n - 1):
        span_copy(slot).start()

    for step in range(2, n - 1):
        arrive_step(step - 1)
        send_step(step)
    arrive_step(n - 2)

    for slot in range(n - 1):
        source = lax.rem(me + n - 1 - slot, n)
        copy_to(
            span_full.at[source],
            span_full.at[source],
            span_send.at[slot],
            span_recv.at[slot],
            tensor_peer(slot + 1),
        ).wait_recv()

    own_copy.wait()
    for slot in range(n - 1):
        sum_copy(slot).wait_send()
        pool_copy(slot).wait_send()
        span_copy(slot).wait_send()
        for copy, valid in (rightward(slot), leftward(slot)):
            pl.when(valid)(copy.wait_send)
    for slot in range(owners - 1):
        owner_copy(slot).wait_send()


def front(
    n, enc_n, req_n, tokens, enc_up, enc_down, enc_gain, proj_weight, selector, reorder, rows
):
    owners = enc_n * req_n
    requests, _, columns = rows.shape
    share = tokens.shape[0] // n
    width = tokens.shape[1]
    slots = requests * CAPR
    vmem = pl.BlockSpec(memory_space=pltpu.VMEM)
    hbm = pl.BlockSpec(memory_space=pl.ANY)
    dma = pltpu.SemaphoreType.DMA
    return pl.pallas_call(
        functools.partial(front_kernel, n, enc_n, req_n),
        out_shape=(
            jax.ShapeDtypeStruct((n, requests, QUESTION_MAX, columns), jnp.bfloat16),
            jax.ShapeDtypeStruct((n, slots * owners, columns), jnp.bfloat16),
        ),
        in_specs=[vmem] * 7 + [hbm],
        out_specs=(hbm, vmem),
        scratch_shapes=[
            pltpu.VMEM((n - 1, share, width), jnp.bfloat16),
            pltpu.VMEM((n - 1, share, width), jnp.bfloat16),
            pltpu.VMEM((share, width), jnp.float32),
            pltpu.VMEM((n, share // SPAN_LEN, width), jnp.bfloat16),
            pltpu.VMEM((owners, slots, width), jnp.bfloat16),
            pltpu.VMEM((owners, slots, width), jnp.bfloat16),
            dma,
        ]
        + [dma((n - 1,))] * 8
        + [dma((owners - 1,))] * 2
        + [dma((n - 1,))] * 2,
        compiler_params=pltpu.CompilerParams(
            collective_id=0, has_side_effects=True, vmem_limit_bytes=40 * 1024 * 1024
        ),
        name="front",
    )(tokens, enc_up, enc_down, enc_gain.reshape(1, -1), proj_weight, selector, reorder, rows)


def project_kernel(
    heads,
    gain,
    question_rows,
    span_rows,
    q_weight,
    k_weight,
    v_weight,
    regroup,
    cosine,
    sines,
    queries,
    kv,
    squares,
    q_sum,
    kv_sum,
):
    step = pl.program_id(0)
    kv_columns = k_weight.shape[1]

    @pl.when(step == 0)
    def _():
        squares[...] = jnp.zeros_like(squares)
        q_sum[...] = jnp.zeros_like(q_sum)
        kv_sum[...] = jnp.zeros_like(kv_sum)

    low = 0
    for part in (question_rows, span_rows):
        size = part.shape[1]
        rows = part[0].astype(jnp.float32)
        squares[low : low + size, :] += jnp.broadcast_to(
            jnp.sum(rows * rows, axis=-1, keepdims=True), (size, squares.shape[1])
        )
        scaled = (rows * gain[0]).astype(jnp.bfloat16)
        q_sum[low : low + size, :] += jnp.dot(
            scaled, q_weight[...], preferred_element_type=jnp.float32
        )
        kv_sum[0, low : low + size, :] += jnp.dot(
            scaled, k_weight[...], preferred_element_type=jnp.float32
        )
        kv_sum[1, low : low + size, :] += jnp.dot(
            scaled, v_weight[...], preferred_element_type=jnp.float32
        )
        low += size

    @pl.when(step == pl.num_programs(0) - 1)
    def _():
        features = gain.shape[2] * pl.num_programs(0)
        scale = lax.rsqrt(squares[...] / features + 1e-05)
        for head in range(heads):
            part = q_sum[:, head * HD : (head + 1) * HD] * scale
            turned = part * cosine[...] + pltpu.roll(part, HD // 2, 1) * sines[...]
            queries[:, head * HD : (head + 1) * HD] = turned.astype(jnp.bfloat16)
        narrow = scale[:, :kv_columns]
        kv[...] = (
            jnp.dot(
                (kv_sum[0] * narrow).astype(jnp.bfloat16),
                regroup[0],
                preferred_element_type=jnp.float32,
            )
            + jnp.dot(
                (kv_sum[1] * narrow).astype(jnp.bfloat16),
                regroup[1],
                preferred_element_type=jnp.float32,
            )
        ).astype(jnp.bfloat16)


def project(question_full, span_full, gain, q_weight, k_weight, v_weight, regroup, cosine, sines):
    n, question_count, columns = question_full.shape
    span_count = span_full.shape[1]
    count = question_count + span_count
    q_columns, kv_columns = q_weight.shape[1], k_weight.shape[1]
    whole = pl.BlockSpec(memory_space=pltpu.VMEM)
    return pl.pallas_call(
        functools.partial(project_kernel, q_columns // HD),
        grid=(n,),
        out_shape=(
            jax.ShapeDtypeStruct((count, q_columns), jnp.bfloat16),
            jax.ShapeDtypeStruct((count, 2 * kv_columns), jnp.bfloat16),
        ),
        in_specs=[
            pl.BlockSpec((1, 1, columns), lambda t: (t, 0, 0)),
            pl.BlockSpec((1, question_count, columns), lambda t: (t, 0, 0)),
            pl.BlockSpec((1, span_count, columns), lambda t: (t, 0, 0)),
            pl.BlockSpec((columns, q_columns), lambda t: (t, 0)),
            pl.BlockSpec((columns, kv_columns), lambda t: (t, 0)),
            pl.BlockSpec((columns, kv_columns), lambda t: (t, 0)),
            whole,
            whole,
            whole,
        ],
        out_specs=(whole, whole),
        scratch_shapes=[
            pltpu.VMEM((count, HD), jnp.float32),
            pltpu.VMEM((count, q_columns), jnp.float32),
            pltpu.VMEM((2, count, kv_columns), jnp.float32),
        ],
        compiler_params=pltpu.CompilerParams(vmem_limit_bytes=48 * 1024 * 1024),
        name="project",
    )(
        gain.reshape(n, 1, columns),
        question_full,
        span_full,
        q_weight,
        k_weight,
        v_weight,
        regroup,
        cosine,
        sines,
    )


def back_kernel(
    n,
    room,
    context,
    o_weight,
    local_rows,
    live_rows,
    out,
    blocks,
    weights,
    total,
    weight_sem,
    right_send,
    right_recv,
    left_send,
    left_recv,
):
    me = lax.axis_index("tensor")
    depth = context.shape[1]
    weight_copy = pltpu.make_async_copy(o_weight, weights, weight_sem)
    weight_copy.start()
    blocks[me] = context[...]

    barrier = pltpu.get_barrier_semaphore()
    for distance in range(1, n):
        pl.semaphore_signal(
            barrier,
            inc=1,
            device_id={"tensor": lax.rem(me + distance, n)},
            device_id_type=pl.DeviceIdType.MESH,
        )
    pl.semaphore_wait(barrier, n - 1)

    def rightward(block, step):
        return copy_to(
            blocks.at[block],
            blocks.at[block],
            right_send.at[step],
            right_recv.at[step],
            {"tensor": jnp.minimum(me + 1, n - 1)},
        )

    def leftward(block, step):
        return copy_to(
            blocks.at[block],
            blocks.at[block],
            left_send.at[step],
            left_recv.at[step],
            {"tensor": jnp.maximum(me - 1, 0)},
        )

    def send_step(step):
        @pl.when(jnp.logical_and(me - step >= 0, me + 1 < n))
        def _():
            rightward(jnp.maximum(me - step, 0), step).start()

        @pl.when(jnp.logical_and(me + step < n, me >= 1))
        def _():
            leftward(jnp.minimum(me + step, n - 1), step).start()

    tile = min(512, out.shape[2])

    def multiply(block):
        rows = pl.ds(pl.multiple_of(block * depth, depth), depth)

        @pl.loop(0, out.shape[2] // tile)
        def _(column):
            at = pl.ds(pl.multiple_of(column * tile, tile), tile)
            total[:, at] += jnp.dot(
                blocks[block], weights[rows, at], preferred_element_type=jnp.float32
            )

    send_step(0)
    total[...] = local_rows[...].astype(jnp.float32)
    weight_copy.wait()
    multiply(me)

    @pl.loop(0, n - 1)
    def _(step):
        left_block = jnp.maximum(me - 1 - step, 0)
        right_block = jnp.minimum(me + 1 + step, n - 1)

        @pl.when(me - 1 - step >= 0)
        def _():
            rightward(left_block, step).wait_recv()

        @pl.when(me + 1 + step < n)
        def _():
            leftward(right_block, step).wait_recv()

        @pl.when(step + 1 < n - 1)
        def _():
            send_step(step + 1)

        @pl.when(me - 1 - step >= 0)
        def _():
            multiply(left_block)

        @pl.when(me + 1 + step < n)
        def _():
            multiply(right_block)

    requests = out.shape[0]
    for request in range(requests):
        rows = slice(request * room, (request + 1) * room)
        kept = total[rows, :] * live_rows[rows, :1]
        rest = jnp.zeros((out.shape[1] - room, out.shape[2]), jnp.float32)
        out[request] = jnp.concatenate([kept, rest], axis=0).astype(jnp.bfloat16)

    @pl.loop(0, n - 1)
    def _(step):
        @pl.when(jnp.logical_and(me - step >= 0, me + 1 < n))
        def _():
            rightward(jnp.maximum(me - step, 0), step).wait_send()

        @pl.when(jnp.logical_and(me + step < n, me >= 1))
        def _():
            leftward(jnp.minimum(me + step, n - 1), step).wait_send()


def back(n, room, context, o_weight, local_rows, live_rows):
    count, depth = context.shape
    columns = o_weight.shape[1]
    vmem = pl.BlockSpec(memory_space=pltpu.VMEM)
    dma = pltpu.SemaphoreType.DMA
    return pl.pallas_call(
        functools.partial(back_kernel, n, room),
        out_shape=jax.ShapeDtypeStruct((count // room, SLOT, columns), jnp.bfloat16),
        in_specs=[vmem, pl.BlockSpec(memory_space=pl.ANY), vmem, vmem],
        out_specs=vmem,
        scratch_shapes=[
            pltpu.VMEM((n, count, depth), jnp.bfloat16),
            pltpu.VMEM(o_weight.shape, jnp.bfloat16),
            pltpu.VMEM((count, columns), jnp.float32),
            dma,
        ]
        + [dma((n - 1,))] * 4,
        compiler_params=pltpu.CompilerParams(
            collective_id=1, has_side_effects=True, vmem_limit_bytes=48 * 1024 * 1024
        ),
        name="back",
    )(context, o_weight, local_rows, live_rows)


def shards(
    span_tokens,
    span_request,
    question_length,
    question_embed,
    enc_up,
    enc_down,
    enc_gain,
    proj_weight,
    norm_gain,
    q_weight,
    k_weight,
    v_weight,
    o_weight,
):
    tensor_count = lax.axis_size("tensor")
    tensor_place = lax.axis_index("tensor")
    owner_count = lax.axis_size(("enc", "req"))
    owner_place = lax.axis_index(("enc", "req"))
    requests_here = question_length.shape[0]
    columns = question_embed.shape[1]
    span_room = CAPR * owner_count
    room = min(SLOT, span_room + QUESTION_MAX)

    question_rows = question_embed.reshape(requests_here, SLOT, columns)
    questions = question_rows[:, :QUESTION_MAX].reshape(-1, columns)

    spans_here = span_tokens.shape[0] // SPAN_LEN
    owners_of = span_request[:, 0]
    all_spans = owners_of.shape[0]
    blocks = owners_of.reshape(owner_count, spans_here)
    index_here = jnp.arange(spans_here, dtype=jnp.int32)
    earlier = index_here[None, :] < index_here[:, None]
    my_spans = lax.dynamic_slice_in_dim(blocks, owner_place, 1, 0)[0]
    same_request = my_spans[None, :] == my_spans[:, None]
    rank_here = jnp.sum(jnp.logical_and(same_request, earlier).astype(jnp.int32), axis=1)
    slot_count = requests_here * CAPR
    placement = my_spans * CAPR + rank_here
    spot_index = jnp.arange(owner_count * slot_count, dtype=jnp.int32)
    selector = (spot_index[:, None] == placement[None, :]).astype(jnp.bfloat16)
    selector = selector.reshape(owner_count, slot_count, tensor_count, -1).swapaxes(1, 2)
    order = jnp.arange(owner_count * slot_count, dtype=jnp.int32)
    from_row = (
        order // CAPR % owner_count * slot_count + order // span_room * CAPR + order % CAPR
    )
    reorder = (from_row[None, :, None] == order.reshape(owner_count, 1, slot_count)).astype(
        jnp.bfloat16
    )
    question_full, span_full = front(
        tensor_count,
        lax.axis_size("enc"),
        lax.axis_size("req"),
        span_tokens,
        enc_up,
        enc_down,
        enc_gain,
        proj_weight,
        selector,
        reorder,
        question_rows,
    )
    span_rows = lax.dynamic_index_in_dim(span_full, tensor_place, 0, keepdims=False)
    question_full = question_full.reshape(tensor_count, -1, columns)

    requests_all = requests_here * owner_count
    exact = all_spans == requests_all * span_room
    local_requests = owner_place * requests_here + jnp.arange(requests_here, dtype=jnp.int32)
    if exact:
        slot_positions = jnp.broadcast_to(
            jnp.arange(room, dtype=jnp.int32)[None, :], (requests_here, room)
        )
        counts = jnp.full((requests_here,), span_room, jnp.int32)
        live = slot_positions < (counts + question_length)[:, None]
    else:
        per_block = jnp.sum(
            (blocks[None, :, :] == local_requests[:, None, None]).astype(jnp.int32), axis=2
        )
        counts = jnp.sum(per_block, axis=1)
        before = jnp.cumsum(per_block, axis=1) - per_block
        rank = jnp.arange(CAPR, dtype=jnp.int32)
        span_positions = (before[:, :, None] + rank[None, None, :]).reshape(requests_here, -1)
        span_live = (rank[None, None, :] < per_block[:, :, None]).reshape(requests_here, -1)
        turn = jnp.arange(QUESTION_MAX, dtype=jnp.int32)
        question_positions = counts[:, None] + turn[None, :]
        question_live = turn[None, :] < question_length[:, None]
        slot_positions = jnp.concatenate([span_positions, question_positions], axis=1)
        live = jnp.concatenate([span_live, question_live], axis=1)

    kv_columns = k_weight.shape[1]
    entries = kv_columns // KVH
    spot = jnp.arange(2 * kv_columns, dtype=jnp.int32)
    head_of, kind_of, entry_of = (
        spot // (2 * entries),
        spot // entries % 2,
        spot % entries,
    )
    regroup = (
        spot[:, None] == (kind_of * kv_columns + entry_of * KVH + head_of)[None, :]
    ).astype(jnp.bfloat16).reshape(2, kv_columns, 2 * kv_columns)
    heads_here = q_weight.shape[1] // HD

    question_slots = requests_here * QUESTION_MAX
    cosine, sines = rope_tables(
        jnp.concatenate(
            [
                slot_positions[:, span_room:].reshape(-1),
                slot_positions[:, :span_room].reshape(-1),
            ]
        )
    )
    queries, kv = project(
        question_full,
        span_full,
        norm_gain,
        q_weight,
        k_weight,
        v_weight,
        regroup,
        jnp.concatenate([cosine, cosine], axis=1),
        jnp.concatenate([-sines, sines], axis=1),
    )

    def by_request(rows):
        return jnp.concatenate(
            [
                rows[question_slots:].reshape(requests_here, span_room, -1),
                rows[:question_slots].reshape(requests_here, QUESTION_MAX, -1),
            ],
            axis=1,
        )

    queries = by_request(queries).reshape(requests_here, -1, heads_here, HD)
    kv = by_request(kv)
    slots = kv.shape[1]
    if tensor_count == KVH:
        kv = kv.reshape(requests_here * slots, KVH, 2 * entries)
        kv = lax.all_to_all(
            jnp.swapaxes(kv, 0, 1), "tensor", split_axis=0, concat_axis=0, tiled=True
        )
        kv = kv.reshape(tensor_count, requests_here, slots, 2, entries)
    else:
        kv = lax.all_gather(kv, "tensor", axis=0, tiled=False)
        kv = kv.reshape(tensor_count, requests_here, slots, KVH, 2, entries)
        shared_head = tensor_place * heads_here // (HQ // KVH)
        kv = lax.dynamic_slice_in_dim(kv, shared_head, 1, 3)[:, :, :, 0]
    kv = jnp.transpose(kv, (3, 1, 2, 0, 4)).reshape(2, requests_here, slots, HD)
    cosine, sines = rope_tables(slot_positions)
    keys = rotate(kv[0].astype(jnp.float32), cosine, sines).astype(jnp.bfloat16)
    values = kv[1]

    local_rows = jnp.concatenate(
        [
            span_rows.reshape(requests_here, span_room, columns),
            questions.reshape(requests_here, QUESTION_MAX, columns),
        ],
        axis=1,
    )
    if not exact:
        at = jnp.arange(room, dtype=jnp.int32)
        order = jnp.logical_and(
            at[None, :, None] == slot_positions[:, None, :], live[:, None, :]
        ).astype(jnp.bfloat16)
        local_rows = jnp.einsum(
            "rps,rsc->rpc", order, local_rows, preferred_element_type=jnp.float32
        ).astype(jnp.bfloat16)
    live_rows = jnp.arange(room, dtype=jnp.int32)[None, :] < (counts + question_length)[:, None]

    scores = jnp.einsum(
        "rphd,rqd->rhpq", queries, keys, preferred_element_type=jnp.float32
    ) * HD ** (-0.5)
    allowed = jnp.logical_and(
        slot_positions[:, :, None] >= slot_positions[:, None, :], live[:, None, :]
    )
    scores = jnp.where(allowed[:, None], scores, -1e30)
    probs = jax.nn.softmax(scores, axis=-1).astype(jnp.bfloat16)
    context = jnp.einsum(
        "rhpq,rqd->rphd", probs, values, preferred_element_type=jnp.float32
    ).astype(jnp.bfloat16)
    context = context.reshape(requests_here, slots, heads_here * HD)
    if not exact:
        context = jnp.einsum(
            "rps,rsc->rpc", order, context, preferred_element_type=jnp.float32
        ).astype(jnp.bfloat16)
    out = back(
        tensor_count,
        room,
        context.reshape(requests_here * room, -1),
        o_weight,
        local_rows.reshape(requests_here * room, columns),
        jnp.broadcast_to(
            live_rows.astype(jnp.float32).reshape(-1, 1), (requests_here * room, 128)
        ),
    )
    return out.reshape(-1, columns)


def solution(mesh):
    return jax.shard_map(
        shards,
        mesh=mesh,
        in_specs=(
            P(("groups", "enc", "req"), None),
            P("groups", None),
            P(("groups", "enc", "req")),
            P(("groups", "enc", "req"), "tensor"),
            P(None, "tensor"),
            P("tensor", None),
            P(),
            P(None, "tensor"),
            P(),
            P(None, "tensor"),
            P(None, "tensor"),
            P(None, "tensor"),
            P(None, "tensor"),
        ),
        out_specs=P(("groups", "enc", "req"), "tensor"),
        check_vma=False,
    )
```

```python
import functools
import math

import jax
import jax.numpy as jnp
from jax import lax
from jax.experimental import pallas as pl
from jax.experimental.pallas import tpu as pltpu
from jax.sharding import PartitionSpec as P

HQ = 32
KVH = 4
HD = 128
SPAN_LEN = 16
SLOT = 64
CAPR = 2
QUESTION_MAX = 32


def rope_tables(positions):
    half_dim = HD // 2
    frequency = jnp.exp(
        jnp.arange(half_dim, dtype=jnp.float32) * (-2.0 * math.log(10000.0) / HD)
    )
    angles = positions.astype(jnp.float32)[..., None] * frequency
    return jnp.cos(angles), jnp.sin(angles)


def rotate(values, cosine, sines):
    half_dim = values.shape[-1] // 2
    lower_half = values[..., :half_dim]
    upper_half = values[..., half_dim:]
    return jnp.concatenate(
        [lower_half * cosine - upper_half * sines, upper_half * cosine + lower_half * sines],
        axis=-1,
    )


def copy_to(src, dst, send_sem, recv_sem, target):
    return pltpu.make_async_remote_copy(
        src_ref=src,
        dst_ref=dst,
        send_sem=send_sem,
        recv_sem=recv_sem,
        device_id=target,
        device_id_type=pl.DeviceIdType.MESH,
    )


def front_kernel(
    n,
    enc_n,
    req_n,
    tokens_hbm,
    up_hbm,
    down_hbm,
    proj_hbm,
    enc_gain,
    selector,
    reorder,
    question_rows,
    question_full,
    span_full,
    tokens,
    enc_up,
    enc_down,
    proj_weight,
    load_sem,
    partial_out,
    partial_in,
    own_sum,
    pooled,
    placed,
    incoming,
    own_sem,
    right_send,
    right_recv,
    left_send,
    left_recv,
    sum_send,
    sum_recv,
    pool_send,
    pool_recv,
    owner_send,
    owner_recv,
    span_send,
    span_recv,
):
    owners = enc_n * req_n
    me = lax.axis_index("tensor")
    my_owner = lax.axis_index("enc") * req_n + lax.axis_index("req")
    share = own_sum.shape[0]
    loads = [
        pltpu.make_async_copy(source, kept, load_sem.at[place])
        for place, (source, kept) in enumerate(
            ((tokens_hbm, tokens), (up_hbm, enc_up), (down_hbm, enc_down), (proj_hbm, proj_weight))
        )
    ]
    for load in loads:
        load.start()

    def tensor_peer(distance):
        return {"tensor": lax.rem(me + distance, n)}

    def owner_peer(distance):
        other = lax.rem(my_owner + distance, owners)
        return other, {"enc": other // req_n, "req": lax.rem(other, req_n)}

    barrier = pltpu.get_barrier_semaphore()
    for distance in range(1, n):
        pl.semaphore_signal(
            barrier,
            inc=1,
            device_id=tensor_peer(distance),
            device_id_type=pl.DeviceIdType.MESH,
        )
    for distance in range(1, owners):
        pl.semaphore_signal(
            barrier,
            inc=1,
            device_id=owner_peer(distance)[1],
            device_id_type=pl.DeviceIdType.MESH,
        )
    pl.semaphore_wait(barrier, n - 1 + owners - 1)

    own_rows = question_rows.at[:, :QUESTION_MAX]
    own_copy = pltpu.make_async_copy(own_rows, question_full.at[me], own_sem)
    own_copy.start()

    def rightward(step):
        block = jnp.maximum(me - step, 0)
        source = own_rows if step == 0 else question_full.at[block]
        copy = copy_to(
            source,
            question_full.at[block],
            right_send.at[step],
            right_recv.at[step],
            {"tensor": jnp.minimum(me + 1, n - 1)},
        )
        return copy, jnp.logical_and(me - step >= 0, me + 1 < n)

    def leftward(step):
        block = jnp.minimum(me + step, n - 1)
        source = own_rows if step == 0 else question_full.at[block]
        copy = copy_to(
            source,
            question_full.at[block],
            left_send.at[step],
            left_recv.at[step],
            {"tensor": jnp.maximum(me - 1, 0)},
        )
        return copy, jnp.logical_and(me + step < n, me >= 1)

    def send_step(step):
        for copy, valid in (rightward(step), leftward(step)):
            pl.when(valid)(copy.start)

    def arrive_step(step):
        @pl.when(me - 1 - step >= 0)
        def _():
            block = jnp.maximum(me - 1 - step, 0)
            copy_to(
                own_rows,
                question_full.at[block],
                right_send.at[step],
                right_recv.at[step],
                {"tensor": jnp.minimum(me + 1, n - 1)},
            ).wait_recv()

        @pl.when(me + 1 + step < n)
        def _():
            block = jnp.minimum(me + 1 + step, n - 1)
            copy_to(
                own_rows,
                question_full.at[block],
                left_send.at[step],
                left_recv.at[step],
                {"tensor": jnp.maximum(me - 1, 0)},
            ).wait_recv()

    send_step(0)

    def term(place):
        rows = tokens[pl.ds(pl.multiple_of(place * share, share), share), :]
        hidden = jnp.dot(rows, enc_up[...], preferred_element_type=jnp.float32)
        hidden = 0.5 * hidden * (1.0 + lax.erf(hidden * math.sqrt(0.5)))
        return jnp.dot(
            hidden.astype(jnp.bfloat16), enc_down[...], preferred_element_type=jnp.float32
        )

    def sum_copy(slot):
        return copy_to(
            partial_out.at[slot],
            partial_in.at[slot],
            sum_send.at[slot],
            sum_recv.at[slot],
            tensor_peer(slot + 1),
        )

    for load in loads[:3]:
        load.wait()

    @pl.loop(0, n - 1)
    def _(slot):
        partial_out[slot] = term(lax.rem(me + slot + 1, n)).astype(jnp.bfloat16)
        sum_copy(slot).start()

    own_tokens = tokens[pl.ds(pl.multiple_of(me * share, share), share), :]
    own_sum[...] = term(me) + own_tokens.astype(jnp.float32)

    if n > 2:
        arrive_step(0)
        send_step(1)

    for slot in range(n - 1):
        sum_copy(slot).wait_recv()
        own_sum[...] += partial_in[slot].astype(jnp.float32)
    summed = own_sum[...]
    center = summed - jnp.mean(summed, axis=-1, keepdims=True)
    spread = jnp.mean(center * center, axis=-1, keepdims=True)
    encoded = center * lax.rsqrt(spread + 1e-05) * enc_gain[...]
    pooled[me] = jnp.mean(
        encoded.reshape(share // SPAN_LEN, SPAN_LEN, encoded.shape[-1]), axis=1
    ).astype(jnp.bfloat16)

    def pool_copy(slot):
        return copy_to(
            pooled.at[me],
            pooled.at[me],
            pool_send.at[slot],
            pool_recv.at[slot],
            tensor_peer(slot + 1),
        )

    for slot in range(n - 1):
        pool_copy(slot).start()
    if n > 3:
        arrive_step(1)
        send_step(2)
    for slot in range(n - 1):
        source = lax.rem(me + n - 1 - slot, n)
        copy_to(
            pooled.at[source],
            pooled.at[source],
            pool_send.at[slot],
            pool_recv.at[slot],
            tensor_peer(slot + 1),
        ).wait_recv()

    for owner in range(owners):
        total = jnp.zeros(placed.shape[1:], jnp.float32)
        for place in range(n):
            total += jnp.dot(
                selector[owner, place], pooled[place], preferred_element_type=jnp.float32
            )
        placed[owner] = total.astype(jnp.bfloat16)
    incoming[my_owner] = placed[my_owner]

    def owner_copy(slot):
        other, target = owner_peer(slot + 1)
        return copy_to(
            placed.at[other],
            incoming.at[my_owner],
            owner_send.at[slot],
            owner_recv.at[slot],
            target,
        )

    for slot in range(owners - 1):
        owner_copy(slot).start()
    for slot in range(owners - 1):
        source = lax.rem(my_owner + owners - 1 - slot, owners)
        copy_to(
            placed.at[source],
            incoming.at[source],
            owner_send.at[slot],
            owner_recv.at[slot],
            owner_peer(slot + 1)[1],
        ).wait_recv()

    ordered = jnp.zeros((span_full.shape[1], incoming.shape[2]), jnp.float32)
    for owner in range(owners):
        ordered += jnp.dot(
            reorder[owner], incoming[owner], preferred_element_type=jnp.float32
        )
    loads[3].wait()
    span_full[me] = jnp.dot(
        ordered.astype(jnp.bfloat16), proj_weight[...], preferred_element_type=jnp.float32
    ).astype(jnp.bfloat16)

    def span_copy(slot):
        return copy_to(
            span_full.at[me],
            span_full.at[me],
            span_send.at[slot],
            span_recv.at[slot],
            tensor_peer(slot + 1),
        )

    for slot in range(n - 1):
        span_copy(slot).start()

    for step in range(3, n - 1):
        arrive_step(step - 1)
        send_step(step)
    arrive_step(n - 2)

    for slot in range(n - 1):
        source = lax.rem(me + n - 1 - slot, n)
        copy_to(
            span_full.at[source],
            span_full.at[source],
            span_send.at[slot],
            span_recv.at[slot],
            tensor_peer(slot + 1),
        ).wait_recv()

    own_copy.wait()
    for slot in range(n - 1):
        sum_copy(slot).wait_send()
        pool_copy(slot).wait_send()
        span_copy(slot).wait_send()
        for copy, valid in (rightward(slot), leftward(slot)):
            pl.when(valid)(copy.wait_send)
    for slot in range(owners - 1):
        owner_copy(slot).wait_send()


def front(
    n, enc_n, req_n, tokens, enc_up, enc_down, enc_gain, proj_weight, selector, reorder, rows
):
    owners = enc_n * req_n
    requests, _, columns = rows.shape
    share = tokens.shape[0] // n
    width = tokens.shape[1]
    slots = requests * CAPR
    vmem = pl.BlockSpec(memory_space=pltpu.VMEM)
    hbm = pl.BlockSpec(memory_space=pl.ANY)
    dma = pltpu.SemaphoreType.DMA
    return pl.pallas_call(
        functools.partial(front_kernel, n, enc_n, req_n),
        out_shape=(
            jax.ShapeDtypeStruct((n, requests, QUESTION_MAX, columns), jnp.bfloat16),
            jax.ShapeDtypeStruct((n, slots * owners, columns), jnp.bfloat16),
        ),
        in_specs=[hbm] * 4 + [vmem] * 3 + [hbm],
        out_specs=(hbm, vmem),
        scratch_shapes=[
            pltpu.VMEM(tokens.shape, jnp.bfloat16),
            pltpu.VMEM(enc_up.shape, jnp.bfloat16),
            pltpu.VMEM(enc_down.shape, jnp.bfloat16),
            pltpu.VMEM(proj_weight.shape, jnp.bfloat16),
            dma((4,)),
            pltpu.VMEM((n - 1, share, width), jnp.bfloat16),
            pltpu.VMEM((n - 1, share, width), jnp.bfloat16),
            pltpu.VMEM((share, width), jnp.float32),
            pltpu.VMEM((n, share // SPAN_LEN, width), jnp.bfloat16),
            pltpu.VMEM((owners, slots, width), jnp.bfloat16),
            pltpu.VMEM((owners, slots, width), jnp.bfloat16),
            dma,
        ]
        + [dma((n - 1,))] * 8
        + [dma((owners - 1,))] * 2
        + [dma((n - 1,))] * 2,
        compiler_params=pltpu.CompilerParams(
            collective_id=0, has_side_effects=True, vmem_limit_bytes=48 * 1024 * 1024
        ),
        name="front",
    )(tokens, enc_up, enc_down, proj_weight, enc_gain.reshape(1, -1), selector, reorder, rows)


def project_kernel(
    heads,
    gain,
    question_rows,
    span_rows,
    q_weight,
    k_weight,
    v_weight,
    regroup,
    cosine,
    sines,
    queries,
    kv,
    squares,
    q_sum,
    kv_sum,
):
    step = pl.program_id(0)
    kv_columns = k_weight.shape[1]

    @pl.when(step == 0)
    def _():
        squares[...] = jnp.zeros_like(squares)
        q_sum[...] = jnp.zeros_like(q_sum)
        kv_sum[...] = jnp.zeros_like(kv_sum)

    low = 0
    for part in (question_rows, span_rows):
        size = part.shape[1]
        rows = part[0].astype(jnp.float32)
        squares[low : low + size, :] += jnp.broadcast_to(
            jnp.sum(rows * rows, axis=-1, keepdims=True), (size, squares.shape[1])
        )
        scaled = (rows * gain[0]).astype(jnp.bfloat16)
        q_sum[low : low + size, :] += jnp.dot(
            scaled, q_weight[...], preferred_element_type=jnp.float32
        )
        kv_sum[0, low : low + size, :] += jnp.dot(
            scaled, k_weight[...], preferred_element_type=jnp.float32
        )
        kv_sum[1, low : low + size, :] += jnp.dot(
            scaled, v_weight[...], preferred_element_type=jnp.float32
        )
        low += size

    @pl.when(step == pl.num_programs(0) - 1)
    def _():
        features = gain.shape[2] * pl.num_programs(0)
        scale = lax.rsqrt(squares[...] / features + 1e-05)
        for head in range(heads):
            part = q_sum[:, head * HD : (head + 1) * HD] * scale
            turned = part * cosine[...] + pltpu.roll(part, HD // 2, 1) * sines[...]
            queries[:, head * HD : (head + 1) * HD] = turned.astype(jnp.bfloat16)
        narrow = scale[:, :kv_columns]
        kv[...] = (
            jnp.dot(
                (kv_sum[0] * narrow).astype(jnp.bfloat16),
                regroup[0],
                preferred_element_type=jnp.float32,
            )
            + jnp.dot(
                (kv_sum[1] * narrow).astype(jnp.bfloat16),
                regroup[1],
                preferred_element_type=jnp.float32,
            )
        ).astype(jnp.bfloat16)


def project(question_full, span_full, gain, q_weight, k_weight, v_weight, regroup, cosine, sines):
    n, question_count, columns = question_full.shape
    span_count = span_full.shape[1]
    count = question_count + span_count
    q_columns, kv_columns = q_weight.shape[1], k_weight.shape[1]
    whole = pl.BlockSpec(memory_space=pltpu.VMEM)
    return pl.pallas_call(
        functools.partial(project_kernel, q_columns // HD),
        grid=(n,),
        out_shape=(
            jax.ShapeDtypeStruct((count, q_columns), jnp.bfloat16),
            jax.ShapeDtypeStruct((count, 2 * kv_columns), jnp.bfloat16),
        ),
        in_specs=[
            pl.BlockSpec((1, 1, columns), lambda t: (t, 0, 0)),
            pl.BlockSpec((1, question_count, columns), lambda t: (t, 0, 0)),
            pl.BlockSpec((1, span_count, columns), lambda t: (t, 0, 0)),
            pl.BlockSpec((columns, q_columns), lambda t: (t, 0)),
            pl.BlockSpec((columns, kv_columns), lambda t: (t, 0)),
            pl.BlockSpec((columns, kv_columns), lambda t: (t, 0)),
            whole,
            whole,
            whole,
        ],
        out_specs=(whole, whole),
        scratch_shapes=[
            pltpu.VMEM((count, HD), jnp.float32),
            pltpu.VMEM((count, q_columns), jnp.float32),
            pltpu.VMEM((2, count, kv_columns), jnp.float32),
        ],
        compiler_params=pltpu.CompilerParams(vmem_limit_bytes=48 * 1024 * 1024),
        name="project",
    )(
        gain.reshape(n, 1, columns),
        question_full,
        span_full,
        q_weight,
        k_weight,
        v_weight,
        regroup,
        cosine,
        sines,
    )


def back_kernel(
    n,
    room,
    context,
    o_weight,
    local_rows,
    live_rows,
    out,
    blocks,
    weights,
    total,
    weight_sem,
    right_send,
    right_recv,
    left_send,
    left_recv,
):
    me = lax.axis_index("tensor")
    depth = context.shape[1]
    weight_copy = pltpu.make_async_copy(o_weight, weights, weight_sem)
    weight_copy.start()
    blocks[me] = context[...]

    barrier = pltpu.get_barrier_semaphore()
    for distance in range(1, n):
        pl.semaphore_signal(
            barrier,
            inc=1,
            device_id={"tensor": lax.rem(me + distance, n)},
            device_id_type=pl.DeviceIdType.MESH,
        )
    pl.semaphore_wait(barrier, n - 1)

    def rightward(block, step):
        return copy_to(
            blocks.at[block],
            blocks.at[block],
            right_send.at[step],
            right_recv.at[step],
            {"tensor": jnp.minimum(me + 1, n - 1)},
        )

    def leftward(block, step):
        return copy_to(
            blocks.at[block],
            blocks.at[block],
            left_send.at[step],
            left_recv.at[step],
            {"tensor": jnp.maximum(me - 1, 0)},
        )

    def send_step(step):
        @pl.when(jnp.logical_and(me - step >= 0, me + 1 < n))
        def _():
            rightward(jnp.maximum(me - step, 0), step).start()

        @pl.when(jnp.logical_and(me + step < n, me >= 1))
        def _():
            leftward(jnp.minimum(me + step, n - 1), step).start()

    tile = min(512, out.shape[2])

    def multiply(block):
        rows = pl.ds(pl.multiple_of(block * depth, depth), depth)

        @pl.loop(0, out.shape[2] // tile)
        def _(column):
            at = pl.ds(pl.multiple_of(column * tile, tile), tile)
            total[:, at] += jnp.dot(
                blocks[block], weights[rows, at], preferred_element_type=jnp.float32
            )

    send_step(0)
    total[...] = local_rows[...].astype(jnp.float32)
    weight_copy.wait()
    multiply(me)

    @pl.loop(0, n - 1)
    def _(step):
        left_block = jnp.maximum(me - 1 - step, 0)
        right_block = jnp.minimum(me + 1 + step, n - 1)

        @pl.when(me - 1 - step >= 0)
        def _():
            rightward(left_block, step).wait_recv()

        @pl.when(me + 1 + step < n)
        def _():
            leftward(right_block, step).wait_recv()

        @pl.when(step + 1 < n - 1)
        def _():
            send_step(step + 1)

        @pl.when(me - 1 - step >= 0)
        def _():
            multiply(left_block)

        @pl.when(me + 1 + step < n)
        def _():
            multiply(right_block)

    requests = out.shape[0]
    for request in range(requests):
        rows = slice(request * room, (request + 1) * room)
        kept = total[rows, :] * live_rows[rows, :1]
        rest = jnp.zeros((out.shape[1] - room, out.shape[2]), jnp.float32)
        out[request] = jnp.concatenate([kept, rest], axis=0).astype(jnp.bfloat16)

    @pl.loop(0, n - 1)
    def _(step):
        @pl.when(jnp.logical_and(me - step >= 0, me + 1 < n))
        def _():
            rightward(jnp.maximum(me - step, 0), step).wait_send()

        @pl.when(jnp.logical_and(me + step < n, me >= 1))
        def _():
            leftward(jnp.minimum(me + step, n - 1), step).wait_send()


def back(n, room, context, o_weight, local_rows, live_rows):
    count, depth = context.shape
    columns = o_weight.shape[1]
    vmem = pl.BlockSpec(memory_space=pltpu.VMEM)
    dma = pltpu.SemaphoreType.DMA
    return pl.pallas_call(
        functools.partial(back_kernel, n, room),
        out_shape=jax.ShapeDtypeStruct((count // room, SLOT, columns), jnp.bfloat16),
        in_specs=[vmem, pl.BlockSpec(memory_space=pl.ANY), vmem, vmem],
        out_specs=vmem,
        scratch_shapes=[
            pltpu.VMEM((n, count, depth), jnp.bfloat16),
            pltpu.VMEM(o_weight.shape, jnp.bfloat16),
            pltpu.VMEM((count, columns), jnp.float32),
            dma,
        ]
        + [dma((n - 1,))] * 4,
        compiler_params=pltpu.CompilerParams(
            collective_id=1, has_side_effects=True, vmem_limit_bytes=48 * 1024 * 1024
        ),
        name="back",
    )(context, o_weight, local_rows, live_rows)


def shards(
    span_tokens,
    span_request,
    question_length,
    question_embed,
    enc_up,
    enc_down,
    enc_gain,
    proj_weight,
    norm_gain,
    q_weight,
    k_weight,
    v_weight,
    o_weight,
):
    tensor_count = lax.axis_size("tensor")
    tensor_place = lax.axis_index("tensor")
    owner_count = lax.axis_size(("enc", "req"))
    owner_place = lax.axis_index(("enc", "req"))
    requests_here = question_length.shape[0]
    columns = question_embed.shape[1]
    span_room = CAPR * owner_count
    room = min(SLOT, span_room + QUESTION_MAX)

    question_rows = question_embed.reshape(requests_here, SLOT, columns)
    questions = question_rows[:, :QUESTION_MAX].reshape(-1, columns)

    spans_here = span_tokens.shape[0] // SPAN_LEN
    owners_of = span_request[:, 0]
    all_spans = owners_of.shape[0]
    blocks = owners_of.reshape(owner_count, spans_here)
    index_here = jnp.arange(spans_here, dtype=jnp.int32)
    earlier = index_here[None, :] < index_here[:, None]
    my_spans = lax.dynamic_slice_in_dim(blocks, owner_place, 1, 0)[0]
    same_request = my_spans[None, :] == my_spans[:, None]
    rank_here = jnp.sum(jnp.logical_and(same_request, earlier).astype(jnp.int32), axis=1)
    slot_count = requests_here * CAPR
    placement = my_spans * CAPR + rank_here
    spot_index = jnp.arange(owner_count * slot_count, dtype=jnp.int32)
    selector = (spot_index[:, None] == placement[None, :]).astype(jnp.bfloat16)
    selector = selector.reshape(owner_count, slot_count, tensor_count, -1).swapaxes(1, 2)
    order = jnp.arange(owner_count * slot_count, dtype=jnp.int32)
    from_row = (
        order // CAPR % owner_count * slot_count + order // span_room * CAPR + order % CAPR
    )
    reorder = (from_row[None, :, None] == order.reshape(owner_count, 1, slot_count)).astype(
        jnp.bfloat16
    )
    question_full, span_full = front(
        tensor_count,
        lax.axis_size("enc"),
        lax.axis_size("req"),
        span_tokens,
        enc_up,
        enc_down,
        enc_gain,
        proj_weight,
        selector,
        reorder,
        question_rows,
    )
    span_rows = lax.dynamic_index_in_dim(span_full, tensor_place, 0, keepdims=False)
    question_full = question_full.reshape(tensor_count, -1, columns)

    requests_all = requests_here * owner_count
    exact = all_spans == requests_all * span_room
    local_requests = owner_place * requests_here + jnp.arange(requests_here, dtype=jnp.int32)
    if exact:
        slot_positions = jnp.broadcast_to(
            jnp.arange(room, dtype=jnp.int32)[None, :], (requests_here, room)
        )
        counts = jnp.full((requests_here,), span_room, jnp.int32)
        live = slot_positions < (counts + question_length)[:, None]
    else:
        per_block = jnp.sum(
            (blocks[None, :, :] == local_requests[:, None, None]).astype(jnp.int32), axis=2
        )
        counts = jnp.sum(per_block, axis=1)
        before = jnp.cumsum(per_block, axis=1) - per_block
        rank = jnp.arange(CAPR, dtype=jnp.int32)
        span_positions = (before[:, :, None] + rank[None, None, :]).reshape(requests_here, -1)
        span_live = (rank[None, None, :] < per_block[:, :, None]).reshape(requests_here, -1)
        turn = jnp.arange(QUESTION_MAX, dtype=jnp.int32)
        question_positions = counts[:, None] + turn[None, :]
        question_live = turn[None, :] < question_length[:, None]
        slot_positions = jnp.concatenate([span_positions, question_positions], axis=1)
        live = jnp.concatenate([span_live, question_live], axis=1)

    kv_columns = k_weight.shape[1]
    entries = kv_columns // KVH
    spot = jnp.arange(2 * kv_columns, dtype=jnp.int32)
    head_of, kind_of, entry_of = (
        spot // (2 * entries),
        spot // entries % 2,
        spot % entries,
    )
    regroup = (
        spot[:, None] == (kind_of * kv_columns + entry_of * KVH + head_of)[None, :]
    ).astype(jnp.bfloat16).reshape(2, kv_columns, 2 * kv_columns)
    heads_here = q_weight.shape[1] // HD

    question_slots = requests_here * QUESTION_MAX
    cosine, sines = rope_tables(
        jnp.concatenate(
            [
                slot_positions[:, span_room:].reshape(-1),
                slot_positions[:, :span_room].reshape(-1),
            ]
        )
    )
    queries, kv = project(
        question_full,
        span_full,
        norm_gain,
        q_weight,
        k_weight,
        v_weight,
        regroup,
        jnp.concatenate([cosine, cosine], axis=1),
        jnp.concatenate([-sines, sines], axis=1),
    )

    def by_request(rows):
        return jnp.concatenate(
            [
                rows[question_slots:].reshape(requests_here, span_room, -1),
                rows[:question_slots].reshape(requests_here, QUESTION_MAX, -1),
            ],
            axis=1,
        )

    queries = by_request(queries).reshape(requests_here, -1, heads_here, HD)
    kv = by_request(kv)
    slots = kv.shape[1]
    if tensor_count == KVH:
        kv = kv.reshape(requests_here * slots, KVH, 2 * entries)
        kv = lax.all_to_all(
            jnp.swapaxes(kv, 0, 1), "tensor", split_axis=0, concat_axis=0, tiled=True
        )
        kv = kv.reshape(tensor_count, requests_here, slots, 2, entries)
    else:
        kv = lax.all_gather(kv, "tensor", axis=0, tiled=False)
        kv = kv.reshape(tensor_count, requests_here, slots, KVH, 2, entries)
        shared_head = tensor_place * heads_here // (HQ // KVH)
        kv = lax.dynamic_slice_in_dim(kv, shared_head, 1, 3)[:, :, :, 0]
    kv = jnp.transpose(kv, (3, 1, 2, 0, 4)).reshape(2, requests_here, slots, HD)
    cosine, sines = rope_tables(slot_positions)
    keys = rotate(kv[0].astype(jnp.float32), cosine, sines).astype(jnp.bfloat16)
    values = kv[1]

    local_rows = jnp.concatenate(
        [
            span_rows.reshape(requests_here, span_room, columns),
            questions.reshape(requests_here, QUESTION_MAX, columns),
        ],
        axis=1,
    )
    if not exact:
        at = jnp.arange(room, dtype=jnp.int32)
        order = jnp.logical_and(
            at[None, :, None] == slot_positions[:, None, :], live[:, None, :]
        ).astype(jnp.bfloat16)
        local_rows = jnp.einsum(
            "rps,rsc->rpc", order, local_rows, preferred_element_type=jnp.float32
        ).astype(jnp.bfloat16)
    live_rows = jnp.arange(room, dtype=jnp.int32)[None, :] < (counts + question_length)[:, None]

    scores = jnp.einsum(
        "rphd,rqd->rhpq", queries, keys, preferred_element_type=jnp.float32
    ) * HD ** (-0.5)
    allowed = jnp.logical_and(
        slot_positions[:, :, None] >= slot_positions[:, None, :], live[:, None, :]
    )
    scores = jnp.where(allowed[:, None], scores, -1e30)
    probs = jax.nn.softmax(scores, axis=-1).astype(jnp.bfloat16)
    context = jnp.einsum(
        "rhpq,rqd->rphd", probs, values, preferred_element_type=jnp.float32
    ).astype(jnp.bfloat16)
    context = context.reshape(requests_here, slots, heads_here * HD)
    if not exact:
        context = jnp.einsum(
            "rps,rsc->rpc", order, context, preferred_element_type=jnp.float32
        ).astype(jnp.bfloat16)
    out = back(
        tensor_count,
        room,
        context.reshape(requests_here * room, -1),
        o_weight,
        local_rows.reshape(requests_here * room, columns),
        jnp.broadcast_to(
            live_rows.astype(jnp.float32).reshape(-1, 1), (requests_here * room, 128)
        ),
    )
    return out.reshape(-1, columns)


def solution(mesh):
    return jax.shard_map(
        shards,
        mesh=mesh,
        in_specs=(
            P(("groups", "enc", "req"), None),
            P("groups", None),
            P(("groups", "enc", "req")),
            P(("groups", "enc", "req"), "tensor"),
            P(None, "tensor"),
            P("tensor", None),
            P(),
            P(None, "tensor"),
            P(),
            P(None, "tensor"),
            P(None, "tensor"),
            P(None, "tensor"),
            P(None, "tensor"),
        ),
        out_specs=P(("groups", "enc", "req"), "tensor"),
        check_vma=False,
    )
```

```python
import functools
import math

import jax
import jax.numpy as jnp
from jax import lax
from jax.experimental import pallas as pl
from jax.experimental.pallas import tpu as pltpu
from jax.sharding import PartitionSpec as P

HQ = 32
KVH = 4
HD = 128
SPAN_LEN = 16
SLOT = 64
CAPR = 2
QUESTION_MAX = 32


def rope_tables(positions):
    half_dim = HD // 2
    frequency = jnp.exp(
        jnp.arange(half_dim, dtype=jnp.float32) * (-2.0 * math.log(10000.0) / HD)
    )
    angles = positions.astype(jnp.float32)[..., None] * frequency
    return jnp.cos(angles), jnp.sin(angles)


def rotate(values, cosine, sines):
    half_dim = values.shape[-1] // 2
    lower_half = values[..., :half_dim]
    upper_half = values[..., half_dim:]
    return jnp.concatenate(
        [lower_half * cosine - upper_half * sines, upper_half * cosine + lower_half * sines],
        axis=-1,
    )


def copy_to(src, dst, send_sem, recv_sem, target):
    return pltpu.make_async_remote_copy(
        src_ref=src,
        dst_ref=dst,
        send_sem=send_sem,
        recv_sem=recv_sem,
        device_id=target,
        device_id_type=pl.DeviceIdType.MESH,
    )


def front_kernel(
    n,
    enc_n,
    req_n,
    tokens_hbm,
    up_hbm,
    down_hbm,
    proj_hbm,
    enc_gain,
    selector,
    reorder,
    question_rows,
    question_full,
    span_full,
    tokens,
    enc_up,
    enc_down,
    proj_weight,
    load_sem,
    partial_out,
    partial_in,
    own_sum,
    pooled,
    placed,
    incoming,
    own_sem,
    right_send,
    right_recv,
    left_send,
    left_recv,
    sum_send,
    sum_recv,
    pool_send,
    pool_recv,
    owner_send,
    owner_recv,
    span_send,
    span_recv,
):
    owners = enc_n * req_n
    me = lax.axis_index("tensor")
    my_owner = lax.axis_index("enc") * req_n + lax.axis_index("req")
    share = own_sum.shape[0]
    loads = [
        pltpu.make_async_copy(source, kept, load_sem.at[place])
        for place, (source, kept) in enumerate(
            ((tokens_hbm, tokens), (up_hbm, enc_up), (down_hbm, enc_down), (proj_hbm, proj_weight))
        )
    ]
    for load in loads:
        load.start()

    def tensor_peer(distance):
        return {"tensor": lax.rem(me + distance, n)}

    def owner_peer(distance):
        other = lax.rem(my_owner + distance, owners)
        return other, {"enc": other // req_n, "req": lax.rem(other, req_n)}

    barrier = pltpu.get_barrier_semaphore()
    for distance in range(1, n):
        pl.semaphore_signal(
            barrier,
            inc=1,
            device_id=tensor_peer(distance),
            device_id_type=pl.DeviceIdType.MESH,
        )
    for distance in range(1, owners):
        pl.semaphore_signal(
            barrier,
            inc=1,
            device_id=owner_peer(distance)[1],
            device_id_type=pl.DeviceIdType.MESH,
        )
    pl.semaphore_wait(barrier, n - 1 + owners - 1)

    own_rows = question_rows.at[:, :QUESTION_MAX]
    own_copy = pltpu.make_async_copy(own_rows, question_full.at[me], own_sem)
    own_copy.start()

    def rightward(step):
        block = jnp.maximum(me - step, 0)
        source = own_rows if step == 0 else question_full.at[block]
        copy = copy_to(
            source,
            question_full.at[block],
            right_send.at[step],
            right_recv.at[step],
            {"tensor": jnp.minimum(me + 1, n - 1)},
        )
        return copy, jnp.logical_and(me - step >= 0, me + 1 < n)

    def leftward(step):
        block = jnp.minimum(me + step, n - 1)
        source = own_rows if step == 0 else question_full.at[block]
        copy = copy_to(
            source,
            question_full.at[block],
            left_send.at[step],
            left_recv.at[step],
            {"tensor": jnp.maximum(me - 1, 0)},
        )
        return copy, jnp.logical_and(me + step < n, me >= 1)

    def send_step(step):
        for copy, valid in (rightward(step), leftward(step)):
            pl.when(valid)(copy.start)

    def arrive_step(step):
        @pl.when(me - 1 - step >= 0)
        def _():
            block = jnp.maximum(me - 1 - step, 0)
            copy_to(
                own_rows,
                question_full.at[block],
                right_send.at[step],
                right_recv.at[step],
                {"tensor": jnp.minimum(me + 1, n - 1)},
            ).wait_recv()

        @pl.when(me + 1 + step < n)
        def _():
            block = jnp.minimum(me + 1 + step, n - 1)
            copy_to(
                own_rows,
                question_full.at[block],
                left_send.at[step],
                left_recv.at[step],
                {"tensor": jnp.maximum(me - 1, 0)},
            ).wait_recv()

    send_step(0)

    def term(place):
        rows = tokens[pl.ds(pl.multiple_of(place * share, share), share), :]
        hidden = jnp.dot(rows, enc_up[...], preferred_element_type=jnp.float32)
        hidden = 0.5 * hidden * (1.0 + lax.erf(hidden * math.sqrt(0.5)))
        return jnp.dot(
            hidden.astype(jnp.bfloat16), enc_down[...], preferred_element_type=jnp.float32
        )

    def sum_copy(slot):
        return copy_to(
            partial_out.at[slot],
            partial_in.at[slot],
            sum_send.at[slot],
            sum_recv.at[slot],
            tensor_peer(slot + 1),
        )

    for load in loads[:3]:
        load.wait()

    @pl.loop(0, n - 1)
    def _(slot):
        partial_out[slot] = term(lax.rem(me + slot + 1, n)).astype(jnp.bfloat16)
        sum_copy(slot).start()

    own_tokens = tokens[pl.ds(pl.multiple_of(me * share, share), share), :]
    own_sum[...] = term(me) + own_tokens.astype(jnp.float32)

    for slot in range(n - 1):
        sum_copy(slot).wait_recv()
        own_sum[...] += partial_in[slot].astype(jnp.float32)
    if n > 2:
        arrive_step(0)
        send_step(1)
    summed = own_sum[...]
    center = summed - jnp.mean(summed, axis=-1, keepdims=True)
    spread = jnp.mean(center * center, axis=-1, keepdims=True)
    encoded = center * lax.rsqrt(spread + 1e-05) * enc_gain[...]
    pooled[me] = jnp.mean(
        encoded.reshape(share // SPAN_LEN, SPAN_LEN, encoded.shape[-1]), axis=1
    ).astype(jnp.bfloat16)

    def pool_copy(slot):
        return copy_to(
            pooled.at[me],
            pooled.at[me],
            pool_send.at[slot],
            pool_recv.at[slot],
            tensor_peer(slot + 1),
        )

    for slot in range(n - 1):
        pool_copy(slot).start()
    for slot in range(n - 1):
        source = lax.rem(me + n - 1 - slot, n)
        copy_to(
            pooled.at[source],
            pooled.at[source],
            pool_send.at[slot],
            pool_recv.at[slot],
            tensor_peer(slot + 1),
        ).wait_recv()

    for owner in range(owners):
        total = jnp.zeros(placed.shape[1:], jnp.float32)
        for place in range(n):
            total += jnp.dot(
                selector[owner, place], pooled[place], preferred_element_type=jnp.float32
            )
        placed[owner] = total.astype(jnp.bfloat16)
    incoming[my_owner] = placed[my_owner]

    def owner_copy(slot):
        other, target = owner_peer(slot + 1)
        return copy_to(
            placed.at[other],
            incoming.at[my_owner],
            owner_send.at[slot],
            owner_recv.at[slot],
            target,
        )

    for slot in range(owners - 1):
        owner_copy(slot).start()
    for slot in range(owners - 1):
        source = lax.rem(my_owner + owners - 1 - slot, owners)
        copy_to(
            placed.at[source],
            incoming.at[source],
            owner_send.at[slot],
            owner_recv.at[slot],
            owner_peer(slot + 1)[1],
        ).wait_recv()

    ordered = jnp.zeros((span_full.shape[1], incoming.shape[2]), jnp.float32)
    for owner in range(owners):
        ordered += jnp.dot(
            reorder[owner], incoming[owner], preferred_element_type=jnp.float32
        )
    loads[3].wait()
    span_full[me] = jnp.dot(
        ordered.astype(jnp.bfloat16), proj_weight[...], preferred_element_type=jnp.float32
    ).astype(jnp.bfloat16)

    def span_copy(slot):
        return copy_to(
            span_full.at[me],
            span_full.at[me],
            span_send.at[slot],
            span_recv.at[slot],
            tensor_peer(slot + 1),
        )

    for slot in range(n - 1):
        span_copy(slot).start()

    for step in range(2, n - 1):
        arrive_step(step - 1)
        send_step(step)
    arrive_step(n - 2)

    for slot in range(n - 1):
        source = lax.rem(me + n - 1 - slot, n)
        copy_to(
            span_full.at[source],
            span_full.at[source],
            span_send.at[slot],
            span_recv.at[slot],
            tensor_peer(slot + 1),
        ).wait_recv()

    own_copy.wait()
    for slot in range(n - 1):
        sum_copy(slot).wait_send()
        pool_copy(slot).wait_send()
        span_copy(slot).wait_send()
        for copy, valid in (rightward(slot), leftward(slot)):
            pl.when(valid)(copy.wait_send)
    for slot in range(owners - 1):
        owner_copy(slot).wait_send()


def front(
    n, enc_n, req_n, tokens, enc_up, enc_down, enc_gain, proj_weight, selector, reorder, rows
):
    owners = enc_n * req_n
    requests, _, columns = rows.shape
    share = tokens.shape[0] // n
    width = tokens.shape[1]
    slots = requests * CAPR
    vmem = pl.BlockSpec(memory_space=pltpu.VMEM)
    hbm = pl.BlockSpec(memory_space=pl.ANY)
    dma = pltpu.SemaphoreType.DMA
    return pl.pallas_call(
        functools.partial(front_kernel, n, enc_n, req_n),
        out_shape=(
            jax.ShapeDtypeStruct((n, requests, QUESTION_MAX, columns), jnp.bfloat16),
            jax.ShapeDtypeStruct((n, slots * owners, columns), jnp.bfloat16),
        ),
        in_specs=[hbm] * 4 + [vmem] * 3 + [hbm],
        out_specs=(hbm, vmem),
        scratch_shapes=[
            pltpu.VMEM(tokens.shape, jnp.bfloat16),
            pltpu.VMEM(enc_up.shape, jnp.bfloat16),
            pltpu.VMEM(enc_down.shape, jnp.bfloat16),
            pltpu.VMEM(proj_weight.shape, jnp.bfloat16),
            dma((4,)),
            pltpu.VMEM((n - 1, share, width), jnp.bfloat16),
            pltpu.VMEM((n - 1, share, width), jnp.bfloat16),
            pltpu.VMEM((share, width), jnp.float32),
            pltpu.VMEM((n, share // SPAN_LEN, width), jnp.bfloat16),
            pltpu.VMEM((owners, slots, width), jnp.bfloat16),
            pltpu.VMEM((owners, slots, width), jnp.bfloat16),
            dma,
        ]
        + [dma((n - 1,))] * 8
        + [dma((owners - 1,))] * 2
        + [dma((n - 1,))] * 2,
        compiler_params=pltpu.CompilerParams(
            collective_id=0, has_side_effects=True, vmem_limit_bytes=48 * 1024 * 1024
        ),
        name="front",
    )(tokens, enc_up, enc_down, proj_weight, enc_gain.reshape(1, -1), selector, reorder, rows)


def project_kernel(
    heads,
    gain,
    question_rows,
    span_rows,
    q_weight,
    k_weight,
    v_weight,
    regroup,
    cosine,
    sines,
    queries,
    kv,
    squares,
    q_sum,
    kv_sum,
):
    step = pl.program_id(0)
    kv_columns = k_weight.shape[1]

    @pl.when(step == 0)
    def _():
        squares[...] = jnp.zeros_like(squares)
        q_sum[...] = jnp.zeros_like(q_sum)
        kv_sum[...] = jnp.zeros_like(kv_sum)

    low = 0
    for part in (question_rows, span_rows):
        size = part.shape[1]
        rows = part[0].astype(jnp.float32)
        squares[low : low + size, :] += jnp.broadcast_to(
            jnp.sum(rows * rows, axis=-1, keepdims=True), (size, squares.shape[1])
        )
        scaled = (rows * gain[0]).astype(jnp.bfloat16)
        q_sum[low : low + size, :] += jnp.dot(
            scaled, q_weight[...], preferred_element_type=jnp.float32
        )
        kv_sum[0, low : low + size, :] += jnp.dot(
            scaled, k_weight[...], preferred_element_type=jnp.float32
        )
        kv_sum[1, low : low + size, :] += jnp.dot(
            scaled, v_weight[...], preferred_element_type=jnp.float32
        )
        low += size

    @pl.when(step == pl.num_programs(0) - 1)
    def _():
        features = gain.shape[2] * pl.num_programs(0)
        scale = lax.rsqrt(squares[...] / features + 1e-05)
        for head in range(heads):
            part = q_sum[:, head * HD : (head + 1) * HD] * scale
            turned = part * cosine[...] + pltpu.roll(part, HD // 2, 1) * sines[...]
            queries[:, head * HD : (head + 1) * HD] = turned.astype(jnp.bfloat16)
        narrow = scale[:, :kv_columns]
        kv[...] = (
            jnp.dot(
                (kv_sum[0] * narrow).astype(jnp.bfloat16),
                regroup[0],
                preferred_element_type=jnp.float32,
            )
            + jnp.dot(
                (kv_sum[1] * narrow).astype(jnp.bfloat16),
                regroup[1],
                preferred_element_type=jnp.float32,
            )
        ).astype(jnp.bfloat16)


def project(question_full, span_full, gain, q_weight, k_weight, v_weight, regroup, cosine, sines):
    n, question_count, columns = question_full.shape
    span_count = span_full.shape[1]
    count = question_count + span_count
    q_columns, kv_columns = q_weight.shape[1], k_weight.shape[1]
    whole = pl.BlockSpec(memory_space=pltpu.VMEM)
    return pl.pallas_call(
        functools.partial(project_kernel, q_columns // HD),
        grid=(n,),
        out_shape=(
            jax.ShapeDtypeStruct((count, q_columns), jnp.bfloat16),
            jax.ShapeDtypeStruct((count, 2 * kv_columns), jnp.bfloat16),
        ),
        in_specs=[
            pl.BlockSpec((1, 1, columns), lambda t: (t, 0, 0)),
            pl.BlockSpec((1, question_count, columns), lambda t: (t, 0, 0)),
            pl.BlockSpec((1, span_count, columns), lambda t: (t, 0, 0)),
            pl.BlockSpec((columns, q_columns), lambda t: (t, 0)),
            pl.BlockSpec((columns, kv_columns), lambda t: (t, 0)),
            pl.BlockSpec((columns, kv_columns), lambda t: (t, 0)),
            whole,
            whole,
            whole,
        ],
        out_specs=(whole, whole),
        scratch_shapes=[
            pltpu.VMEM((count, HD), jnp.float32),
            pltpu.VMEM((count, q_columns), jnp.float32),
            pltpu.VMEM((2, count, kv_columns), jnp.float32),
        ],
        compiler_params=pltpu.CompilerParams(vmem_limit_bytes=48 * 1024 * 1024),
        name="project",
    )(
        gain.reshape(n, 1, columns),
        question_full,
        span_full,
        q_weight,
        k_weight,
        v_weight,
        regroup,
        cosine,
        sines,
    )


def back_kernel(
    n,
    room,
    context,
    o_weight,
    local_rows,
    live_rows,
    out,
    blocks,
    weights,
    total,
    weight_sem,
    right_send,
    right_recv,
    left_send,
    left_recv,
):
    me = lax.axis_index("tensor")
    depth = context.shape[1]
    weight_copy = pltpu.make_async_copy(o_weight, weights, weight_sem)
    weight_copy.start()
    blocks[me] = context[...]

    barrier = pltpu.get_barrier_semaphore()
    for distance in range(1, n):
        pl.semaphore_signal(
            barrier,
            inc=1,
            device_id={"tensor": lax.rem(me + distance, n)},
            device_id_type=pl.DeviceIdType.MESH,
        )
    pl.semaphore_wait(barrier, n - 1)

    def rightward(block, step):
        return copy_to(
            blocks.at[block],
            blocks.at[block],
            right_send.at[step],
            right_recv.at[step],
            {"tensor": jnp.minimum(me + 1, n - 1)},
        )

    def leftward(block, step):
        return copy_to(
            blocks.at[block],
            blocks.at[block],
            left_send.at[step],
            left_recv.at[step],
            {"tensor": jnp.maximum(me - 1, 0)},
        )

    def send_step(step):
        @pl.when(jnp.logical_and(me - step >= 0, me + 1 < n))
        def _():
            rightward(jnp.maximum(me - step, 0), step).start()

        @pl.when(jnp.logical_and(me + step < n, me >= 1))
        def _():
            leftward(jnp.minimum(me + step, n - 1), step).start()

    tile = min(512, out.shape[2])

    def multiply(block):
        rows = pl.ds(pl.multiple_of(block * depth, depth), depth)

        @pl.loop(0, out.shape[2] // tile)
        def _(column):
            at = pl.ds(pl.multiple_of(column * tile, tile), tile)
            total[:, at] += jnp.dot(
                blocks[block], weights[rows, at], preferred_element_type=jnp.float32
            )

    send_step(0)
    total[...] = local_rows[...].astype(jnp.float32)
    weight_copy.wait()
    multiply(me)

    @pl.loop(0, n - 1)
    def _(step):
        left_block = jnp.maximum(me - 1 - step, 0)
        right_block = jnp.minimum(me + 1 + step, n - 1)

        @pl.when(me - 1 - step >= 0)
        def _():
            rightward(left_block, step).wait_recv()

        @pl.when(me + 1 + step < n)
        def _():
            leftward(right_block, step).wait_recv()

        @pl.when(step + 1 < n - 1)
        def _():
            send_step(step + 1)

        @pl.when(me - 1 - step >= 0)
        def _():
            multiply(left_block)

        @pl.when(me + 1 + step < n)
        def _():
            multiply(right_block)

    requests = out.shape[0]
    for request in range(requests):
        rows = slice(request * room, (request + 1) * room)
        kept = total[rows, :] * live_rows[rows, :1]
        rest = jnp.zeros((out.shape[1] - room, out.shape[2]), jnp.float32)
        out[request] = jnp.concatenate([kept, rest], axis=0).astype(jnp.bfloat16)

    @pl.loop(0, n - 1)
    def _(step):
        @pl.when(jnp.logical_and(me - step >= 0, me + 1 < n))
        def _():
            rightward(jnp.maximum(me - step, 0), step).wait_send()

        @pl.when(jnp.logical_and(me + step < n, me >= 1))
        def _():
            leftward(jnp.minimum(me + step, n - 1), step).wait_send()


def back(n, room, context, o_weight, local_rows, live_rows):
    count, depth = context.shape
    columns = o_weight.shape[1]
    vmem = pl.BlockSpec(memory_space=pltpu.VMEM)
    dma = pltpu.SemaphoreType.DMA
    return pl.pallas_call(
        functools.partial(back_kernel, n, room),
        out_shape=jax.ShapeDtypeStruct((count // room, SLOT, columns), jnp.bfloat16),
        in_specs=[vmem, pl.BlockSpec(memory_space=pl.ANY), vmem, vmem],
        out_specs=vmem,
        scratch_shapes=[
            pltpu.VMEM((n, count, depth), jnp.bfloat16),
            pltpu.VMEM(o_weight.shape, jnp.bfloat16),
            pltpu.VMEM((count, columns), jnp.float32),
            dma,
        ]
        + [dma((n - 1,))] * 4,
        compiler_params=pltpu.CompilerParams(
            collective_id=1, has_side_effects=True, vmem_limit_bytes=48 * 1024 * 1024
        ),
        name="back",
    )(context, o_weight, local_rows, live_rows)


def shards(
    span_tokens,
    span_request,
    question_length,
    question_embed,
    enc_up,
    enc_down,
    enc_gain,
    proj_weight,
    norm_gain,
    q_weight,
    k_weight,
    v_weight,
    o_weight,
):
    tensor_count = lax.axis_size("tensor")
    tensor_place = lax.axis_index("tensor")
    owner_count = lax.axis_size(("enc", "req"))
    owner_place = lax.axis_index(("enc", "req"))
    requests_here = question_length.shape[0]
    columns = question_embed.shape[1]
    span_room = CAPR * owner_count
    room = min(SLOT, span_room + QUESTION_MAX)

    question_rows = question_embed.reshape(requests_here, SLOT, columns)
    questions = question_rows[:, :QUESTION_MAX].reshape(-1, columns)

    spans_here = span_tokens.shape[0] // SPAN_LEN
    owners_of = span_request[:, 0]
    all_spans = owners_of.shape[0]
    blocks = owners_of.reshape(owner_count, spans_here)
    index_here = jnp.arange(spans_here, dtype=jnp.int32)
    earlier = index_here[None, :] < index_here[:, None]
    my_spans = lax.dynamic_slice_in_dim(blocks, owner_place, 1, 0)[0]
    same_request = my_spans[None, :] == my_spans[:, None]
    rank_here = jnp.sum(jnp.logical_and(same_request, earlier).astype(jnp.int32), axis=1)
    slot_count = requests_here * CAPR
    placement = my_spans * CAPR + rank_here
    spot_index = jnp.arange(owner_count * slot_count, dtype=jnp.int32)
    selector = (spot_index[:, None] == placement[None, :]).astype(jnp.bfloat16)
    selector = selector.reshape(owner_count, slot_count, tensor_count, -1).swapaxes(1, 2)
    order = jnp.arange(owner_count * slot_count, dtype=jnp.int32)
    from_row = (
        order // CAPR % owner_count * slot_count + order // span_room * CAPR + order % CAPR
    )
    reorder = (from_row[None, :, None] == order.reshape(owner_count, 1, slot_count)).astype(
        jnp.bfloat16
    )
    question_full, span_full = front(
        tensor_count,
        lax.axis_size("enc"),
        lax.axis_size("req"),
        span_tokens,
        enc_up,
        enc_down,
        enc_gain,
        proj_weight,
        selector,
        reorder,
        question_rows,
    )
    span_rows = lax.dynamic_index_in_dim(span_full, tensor_place, 0, keepdims=False)
    question_full = question_full.reshape(tensor_count, -1, columns)

    requests_all = requests_here * owner_count
    exact = all_spans == requests_all * span_room
    local_requests = owner_place * requests_here + jnp.arange(requests_here, dtype=jnp.int32)
    if exact:
        slot_positions = jnp.broadcast_to(
            jnp.arange(room, dtype=jnp.int32)[None, :], (requests_here, room)
        )
        counts = jnp.full((requests_here,), span_room, jnp.int32)
        live = slot_positions < (counts + question_length)[:, None]
    else:
        per_block = jnp.sum(
            (blocks[None, :, :] == local_requests[:, None, None]).astype(jnp.int32), axis=2
        )
        counts = jnp.sum(per_block, axis=1)
        before = jnp.cumsum(per_block, axis=1) - per_block
        rank = jnp.arange(CAPR, dtype=jnp.int32)
        span_positions = (before[:, :, None] + rank[None, None, :]).reshape(requests_here, -1)
        span_live = (rank[None, None, :] < per_block[:, :, None]).reshape(requests_here, -1)
        turn = jnp.arange(QUESTION_MAX, dtype=jnp.int32)
        question_positions = counts[:, None] + turn[None, :]
        question_live = turn[None, :] < question_length[:, None]
        slot_positions = jnp.concatenate([span_positions, question_positions], axis=1)
        live = jnp.concatenate([span_live, question_live], axis=1)

    kv_columns = k_weight.shape[1]
    entries = kv_columns // KVH
    spot = jnp.arange(2 * kv_columns, dtype=jnp.int32)
    head_of, kind_of, entry_of = (
        spot // (2 * entries),
        spot // entries % 2,
        spot % entries,
    )
    regroup = (
        spot[:, None] == (kind_of * kv_columns + entry_of * KVH + head_of)[None, :]
    ).astype(jnp.bfloat16).reshape(2, kv_columns, 2 * kv_columns)
    heads_here = q_weight.shape[1] // HD

    question_slots = requests_here * QUESTION_MAX
    cosine, sines = rope_tables(
        jnp.concatenate(
            [
                slot_positions[:, span_room:].reshape(-1),
                slot_positions[:, :span_room].reshape(-1),
            ]
        )
    )
    queries, kv = project(
        question_full,
        span_full,
        norm_gain,
        q_weight,
        k_weight,
        v_weight,
        regroup,
        jnp.concatenate([cosine, cosine], axis=1),
        jnp.concatenate([-sines, sines], axis=1),
    )

    def by_request(rows):
        return jnp.concatenate(
            [
                rows[question_slots:].reshape(requests_here, span_room, -1),
                rows[:question_slots].reshape(requests_here, QUESTION_MAX, -1),
            ],
            axis=1,
        )

    queries = by_request(queries).reshape(requests_here, -1, heads_here, HD)
    kv = by_request(kv)
    slots = kv.shape[1]
    if tensor_count == KVH:
        kv = kv.reshape(requests_here * slots, KVH, 2 * entries)
        kv = lax.all_to_all(
            jnp.swapaxes(kv, 0, 1), "tensor", split_axis=0, concat_axis=0, tiled=True
        )
        kv = kv.reshape(tensor_count, requests_here, slots, 2, entries)
    else:
        kv = lax.all_gather(kv, "tensor", axis=0, tiled=False)
        kv = kv.reshape(tensor_count, requests_here, slots, KVH, 2, entries)
        shared_head = tensor_place * heads_here // (HQ // KVH)
        kv = lax.dynamic_slice_in_dim(kv, shared_head, 1, 3)[:, :, :, 0]
    kv = jnp.transpose(kv, (3, 1, 2, 0, 4)).reshape(2, requests_here, slots, HD)
    cosine, sines = rope_tables(slot_positions)
    keys = rotate(kv[0].astype(jnp.float32), cosine, sines).astype(jnp.bfloat16)
    values = kv[1]

    local_rows = jnp.concatenate(
        [
            span_rows.reshape(requests_here, span_room, columns),
            questions.reshape(requests_here, QUESTION_MAX, columns),
        ],
        axis=1,
    )
    if not exact:
        at = jnp.arange(room, dtype=jnp.int32)
        order = jnp.logical_and(
            at[None, :, None] == slot_positions[:, None, :], live[:, None, :]
        ).astype(jnp.bfloat16)
        local_rows = jnp.einsum(
            "rps,rsc->rpc", order, local_rows, preferred_element_type=jnp.float32
        ).astype(jnp.bfloat16)
    live_rows = jnp.arange(room, dtype=jnp.int32)[None, :] < (counts + question_length)[:, None]

    scores = jnp.einsum(
        "rphd,rqd->rhpq", queries, keys, preferred_element_type=jnp.float32
    ) * HD ** (-0.5)
    allowed = jnp.logical_and(
        slot_positions[:, :, None] >= slot_positions[:, None, :], live[:, None, :]
    )
    scores = jnp.where(allowed[:, None], scores, -1e30)
    probs = jax.nn.softmax(scores, axis=-1).astype(jnp.bfloat16)
    context = jnp.einsum(
        "rhpq,rqd->rphd", probs, values, preferred_element_type=jnp.float32
    ).astype(jnp.bfloat16)
    context = context.reshape(requests_here, slots, heads_here * HD)
    if not exact:
        context = jnp.einsum(
            "rps,rsc->rpc", order, context, preferred_element_type=jnp.float32
        ).astype(jnp.bfloat16)
    out = back(
        tensor_count,
        room,
        context.reshape(requests_here * room, -1),
        o_weight,
        local_rows.reshape(requests_here * room, columns),
        jnp.broadcast_to(
            live_rows.astype(jnp.float32).reshape(-1, 1), (requests_here * room, 128)
        ),
    )
    return out.reshape(-1, columns)


def solution(mesh):
    return jax.shard_map(
        shards,
        mesh=mesh,
        in_specs=(
            P(("groups", "enc", "req"), None),
            P("groups", None),
            P(("groups", "enc", "req")),
            P(("groups", "enc", "req"), "tensor"),
            P(None, "tensor"),
            P("tensor", None),
            P(),
            P(None, "tensor"),
            P(),
            P(None, "tensor"),
            P(None, "tensor"),
            P(None, "tensor"),
            P(None, "tensor"),
        ),
        out_specs=P(("groups", "enc", "req"), "tensor"),
        check_vma=False,
    )
```
